512 devices in a mesh: inner: 32 (over z_hi, y), outer: 4 (over x), heads: 4 (over z_lo, core).
Axes of the slice: x: 4, y: 8, z: 8 (z_hi: 4, z_lo: 2; z = z_hi * 2 + z_lo), core: 2. Of those that a mesh axis runs over, the one named last changes fastest.
Arguments:
- q_raw: bfloat16 [16384, 64, 128], P(('inner', 'outer'), 'heads'), may hold values from -6 to 6
- k_raw: bfloat16 [16384, 8, 128], P(('inner', 'outer'), 'heads'), may hold values from -6 to 6
- values: bfloat16 [16384, 8, 128], P(('inner', 'outer'), 'heads'), may hold values from -6 to 6
- attn_out: bfloat16 [16384, 64, 128], P(('inner', 'outer'), 'heads'), may hold values from -1.796875 to 1.796875
- d_out: bfloat16 [16384, 64, 128], P(('inner', 'outer'), 'heads'), may hold values from -24 to 24
- lse: float32 [64, 16384], P('heads', ('inner', 'outer')), may hold values from 1 to 12
- q_gain: float32 [128], replicated, may hold values from 0.5 to 1.5
- k_gain: float32 [128], replicated, may hold values from 0.5 to 1.5
- span_order: int32 [256], replicated, may hold values from 0 to 255, as said below
Outputs:
- d_q_raw: bfloat16 [16384, 64, 128], P(('inner', 'outer'), 'heads')
- d_k_raw: bfloat16 [16384, 8, 128], P(('inner', 'outer'), 'heads')
- d_values: bfloat16 [16384, 8, 128], P(('inner', 'outer'), 'heads')
- d_q_gain: float32 [128], replicated
- d_k_gain: float32 [128], replicated
The draws below stay inside these ranges and needn't reach their ends.
Inputs may be any that keep to these rules, and one draw needn't show every extreme that they name: `span_order`: for one whole number c0 of the draw, slots 2 b and 2 b + 1 hold spans c and 255 - c, in one order or the other for all b alike, with c = (b + c0) mod 128; so block b holds one early and one late span.
All inputs are finite; a program needn't handle non-finite values.
Results may differ from the reference program's by a relative error of at most 0.018.
The reference program's roundings to bfloat16 on the way count: a program that leaves them out, or rounds other values in their place, can miss the bound.
Values may be sent and summed in bfloat16 or wider, within the bound.
No kernel may reach another device: no remote copies, remote signals or barrier semaphores. Data moves between devices by JAX's collectives and lax.ppermute only.
A program may use at most 64 MiB of HBM per device.

```python
import jax
import jax.numpy as jnp
from jax import lax

QH = 64
KVH = 8
DH = 128
TOK_DEV = 128
WINDOW = 5
SPAN = 64
CYCLE = 128
SPANS = 256
SEQ = 16384


def shared_order(key):
    offset = jax.random.randint(jax.random.fold_in(key, 17), (), 0, CYCLE, dtype=jnp.int32)
    flipped = jax.random.randint(jax.random.fold_in(key, 19), (), 0, 2, dtype=jnp.int32)
    blocks = jnp.arange(CYCLE, dtype=jnp.int32)
    early = (blocks + offset) % CYCLE
    late = SPANS - 1 - early
    first = jnp.where(flipped == 1, late, early)
    second = jnp.where(flipped == 1, early, late)
    return jnp.stack([first, second], axis=1).reshape(SPANS).astype(jnp.int32)


def draw_span_order(key, part):
    span_ids = shared_order(key)
    return span_ids


def draw_lse(key, part):
    span_ids = shared_order(key)
    key = jax.random.fold_in(key, 5)
    rows_all = jnp.arange(SEQ, dtype=jnp.int32)
    positions = span_ids[rows_all // SPAN] * SPAN + rows_all % SPAN
    device = rows_all // TOK_DEV
    visible_count = jnp.zeros((SEQ,), jnp.int32)
    for hop_step in range(WINDOW):
        source = (device - hop_step) % CYCLE
        for which in range(2):
            starts = span_ids[2 * source + which] * SPAN
            visible_count = visible_count + jnp.clip(positions - starts + 1, 0, SPAN)
    baseline = jnp.log(1.5 * visible_count.astype(jnp.float32) + SPAN) + 0.5
    noise = 0.3 * jax.random.truncated_normal(key, -2.0, 2.0, (QH, SEQ), jnp.float32)
    return baseline[None, :] + noise


def block_scale(rng, dims, split, least, high):
    def one(position, parts):
        steps = jax.random.uniform(jax.random.fold_in(jax.random.fold_in(rng, 6), position), (parts,), jnp.float32, least / len(split), high / len(split))
        return jnp.repeat(jnp.exp(steps), dims[position] // parts).reshape((-1,) + (1,) * (len(dims) - position - 1))

    gain = one(*split[0])
    for cut in split[1:]:
        gain = gain * one(*cut)
    return gain


def bell_draw(own_key, extent, spread, bound, pieces=(), kind=jnp.bfloat16):
    loudness = block_scale(own_key, extent, pieces, -0.22, 0.18) if pieces else 1.0
    result = jax.random.normal(own_key, extent, jnp.float32) * spread * loudness
    return jnp.minimum(jnp.maximum(result, -bound), bound).astype(kind)


def setup_inputs(seed: int = 0) -> dict:
    arg_keys = jax.random.split(jax.random.key(seed), 10)
    return {
        "q_raw": bell_draw(arg_keys[0], (SEQ, QH, DH), 1.0, 6.0, ((0, 128), (1, 4))),
        "k_raw": bell_draw(arg_keys[1], (SEQ, KVH, DH), 1.0, 6.0, ((0, 128), (1, 4))),
        "values": bell_draw(arg_keys[2], (SEQ, KVH, DH), 1.0, 6.0, ((0, 128), (1, 4))),
        "attn_out": bell_draw(arg_keys[3], (SEQ, QH, DH), 0.3, 1.796875, ((0, 128), (1, 4))),
        "d_out": bell_draw(arg_keys[4], (SEQ, QH, DH), 4.0, 24.0, ((0, 128), (1, 4))),
        "lse": draw_lse(jax.random.fold_in(arg_keys[9], 71), 0),
        "q_gain": jnp.clip(1.0 + 0.1 * jax.random.normal(arg_keys[6], (DH,), jnp.float32), 0.5, 1.5),
        "k_gain": jnp.clip(1.0 + 0.1 * jax.random.normal(arg_keys[7], (DH,), jnp.float32), 0.5, 1.5),
        "span_order": draw_span_order(jax.random.fold_in(arg_keys[9], 71), 0),
    }


EPSILON = 1e-06

def normalize(raw_rows, gain_row):
    floats = raw_rows.astype(jnp.float32)
    inverse = lax.rsqrt(lax.optimization_barrier(jnp.mean(floats * floats, axis=-1, keepdims=True)) + EPSILON)
    unit_rows = floats * inverse
    return (unit_rows, inverse, (unit_rows * gain_row).astype(jnp.bfloat16))

def norm_backward(unit_rows, inverse, gain_row, gradient):
    scaled = gradient * gain_row
    projected = lax.optimization_barrier(jnp.mean(scaled * unit_rows, axis=-1, keepdims=True))
    raw_grad = ((scaled - unit_rows * projected) * inverse).astype(jnp.bfloat16)
    return (raw_grad, lax.optimization_barrier(jnp.sum(gradient * unit_rows, axis=(0, 1))))

def slot_positions(span_order):
    rows_all = jnp.arange(SEQ, dtype=jnp.int32)
    return span_order[rows_all // SPAN] * SPAN + rows_all % SPAN

def reference(q_raw, k_raw, values, attn_out, d_out, lse, q_gain, k_gain, span_order):
    members = QH // KVH
    score_scale = DH ** (-0.5)
    unit_q, inverse_q, q_normed = normalize(q_raw, q_gain)
    unit_k, inverse_k, k_normed = normalize(k_raw, k_gain)
    row_delta = lax.optimization_barrier(jnp.sum(d_out.astype(jnp.float32) * attn_out.astype(jnp.float32), axis=-1))
    positions = slot_positions(span_order).reshape(CYCLE, TOK_DEV)
    q_blocks = q_normed.reshape(CYCLE, TOK_DEV, KVH, members, DH)
    out_blocks = d_out.reshape(CYCLE, TOK_DEV, KVH, members, DH)
    lse_blocks = lse.reshape(KVH, members, CYCLE, TOK_DEV).transpose(2, 0, 1, 3)
    delta_blocks = row_delta.T.reshape(KVH, members, CYCLE, TOK_DEV).transpose(2, 0, 1, 3)
    key_blocks = k_normed.reshape(CYCLE, TOK_DEV, KVH, DH)
    value_blocks = values.reshape(CYCLE, TOK_DEV, KVH, DH)

    def visit(carry, place):
        key_grads, value_grads = carry
        queries = lax.dynamic_index_in_dim(q_blocks, place, 0, keepdims=False).astype(jnp.float32)
        grads_out = lax.dynamic_index_in_dim(out_blocks, place, 0, keepdims=False).astype(jnp.float32)
        lse_rows = lax.dynamic_index_in_dim(lse_blocks, place, 0, keepdims=False)
        delta_rows = lax.dynamic_index_in_dim(delta_blocks, place, 0, keepdims=False)
        query_pos = lax.dynamic_index_in_dim(positions, place, 0, keepdims=False)
        d_query = jnp.zeros((TOK_DEV, KVH, members, DH), jnp.float32)
        for hop_step in range(WINDOW):
            source = ((place - hop_step) % CYCLE).astype(jnp.int32)
            key_block = lax.dynamic_index_in_dim(key_blocks, source, 0, keepdims=False).astype(jnp.float32)
            value_block = lax.dynamic_index_in_dim(value_blocks, source, 0, keepdims=False).astype(jnp.float32)
            key_pos = lax.dynamic_index_in_dim(positions, source, 0, keepdims=False)
            visible = key_pos[None, :] <= query_pos[:, None]
            scores = jnp.einsum('qhgd,khd->hgqk', queries, key_block) * score_scale
            probs = jnp.where(visible, jnp.exp(scores - lse_rows[..., None]), 0.0)
            probs_low = probs.astype(jnp.bfloat16).astype(jnp.float32)
            d_probs = jnp.einsum('qhgd,khd->hgqk', grads_out, value_block)
            d_scores = (probs * (d_probs - delta_rows[..., None])).astype(jnp.bfloat16).astype(jnp.float32)
            d_query = d_query + jnp.einsum('hgqk,khd->qhgd', d_scores, key_block) * score_scale
            d_key = jnp.einsum('hgqk,qhgd->khd', d_scores, queries) * score_scale
            d_value = jnp.einsum('hgqk,qhgd->khd', probs_low, grads_out)
            key_grads = key_grads.at[source].add(d_key)
            value_grads = value_grads.at[source].add(d_value)
        return ((key_grads, value_grads), d_query)
    zeros = jnp.zeros((CYCLE, TOK_DEV, KVH, DH), jnp.float32)
    (key_grads, value_grads), d_query = lax.scan(visit, (zeros, zeros), jnp.arange(CYCLE, dtype=jnp.int32))
    d_q_raw, d_q_gain = norm_backward(unit_q, inverse_q, q_gain, d_query.reshape(SEQ, QH, DH))
    d_k_raw, d_k_gain = norm_backward(unit_k, inverse_k, k_gain, key_grads.reshape(SEQ, KVH, DH))
    d_values = value_grads.reshape(SEQ, KVH, DH).astype(jnp.bfloat16)
    return (d_q_raw, d_k_raw, d_values, d_q_gain, d_k_gain)
```

```python
import jax
import jax.numpy as jnp
import numpy as np
from jax import lax
from jax.experimental import pallas as pl
from jax.experimental.pallas import tpu as pltpu
from jax.sharding import PartitionSpec as P

F32 = jnp.float32
BF16 = jnp.bfloat16
EPSILON = 1e-06
TOK = 128
HALF = 64
KV = 2
MEM = 8
DH = 128
ROWS = HALF * MEM
SLOTS = 4
SCALE = DH ** (-0.5)
LOG2E = float(np.log2(np.e))
PAYLOAD = 2 * TOK * KV
EXTRA = 16
VMEM = pl.BlockSpec(memory_space=pltpu.VMEM)
SMEM = pl.BlockSpec(memory_space=pltpu.SMEM)
PARAMS = pltpu.CompilerParams(vmem_limit_bytes=32 * 1024 * 1024)


def dot_nt(a, b):
    return lax.dot_general(a, b, (((1,), (1,)), ((), ())), preferred_element_type=F32)


def dot_nn(a, b):
    return lax.dot_general(a, b, (((1,), (0,)), ((), ())), preferred_element_type=F32)


def dot_tn(a, b):
    return lax.dot_general(a, b, (((0,), (0,)), ((), ())), preferred_element_type=F32)


def unit_of(floats):
    inverse = lax.rsqrt(jnp.mean(floats * floats, axis=-1, keepdims=True) + EPSILON)
    return floats * inverse, inverse


def norm_backward(unit, inverse, gain, gradient):
    scaled = gradient * gain
    projected = jnp.mean(scaled * unit, axis=-1, keepdims=True)
    return (scaled - unit * projected) * inverse


def pair(key, value, query, grad_out, lse2, delta, mask=None):
    scores = dot_nt(key, query)
    probs = jnp.exp2(scores * (SCALE * LOG2E) - lse2)
    if mask is not None:
        probs = jnp.where(mask, probs, 0.0)
    d_probs = dot_nt(value, grad_out)
    d_scores = (probs * (d_probs - delta)).astype(BF16)
    d_value = dot_nn(probs.astype(BF16), grad_out)
    d_key = dot_nn(d_scores, query) * SCALE
    d_query = dot_tn(d_scores, key) * SCALE
    return d_query, d_key, d_value


def split(scratch, at, group):
    first = scratch[at, pl.ds(group, HALF, stride=KV), :].astype(BF16)
    second = scratch[at, pl.ds(TOK + group, HALF, stride=KV), :].astype(BF16)
    return first, second


def prep_kernel(info, q_raw, d_out, attn_out, lse2, k_raw, values, q_gain, k_gain,
                q_norm, grads_out, delta, d_query, d_local, k_part, keys):
    flip = info[0]
    flipped = flip == 1
    gain = q_gain[...]
    ones = jnp.ones((8, DH), F32)
    for group in range(KV):
        q_rows = q_raw[...].astype(F32)[:, group * MEM:(group + 1) * MEM, :]
        unit, _ = unit_of(q_rows.reshape(TOK * MEM, DH))
        normed = (unit * gain).astype(BF16)
        grads = d_out[...].astype(F32)[:, group * MEM:(group + 1) * MEM, :].reshape(TOK * MEM, DH)
        outs = attn_out[...].astype(F32)[:, group * MEM:(group + 1) * MEM, :].reshape(TOK * MEM, DH)
        row_delta = lax.dot_general(ones, grads * outs, (((1,), (1,)), ((), ())),
                                    precision=lax.Precision.HIGHEST, preferred_element_type=F32)
        grads = grads.astype(BF16)
        for half in range(2):
            rows = slice(half * ROWS, (half + 1) * ROWS)
            q_norm[group, half] = normed[rows]
            grads_out[group, half] = grads[rows]
            delta[group, half] = row_delta[0:1, rows]

    k_unit, _ = unit_of(k_raw[...].astype(F32))
    keys[0] = (k_unit * k_gain[...]).astype(BF16).astype(F32)
    keys[1] = values[...].astype(F32)
    key_at = lax.broadcasted_iota(jnp.int32, (HALF, ROWS), 0)
    query_at = lax.broadcasted_iota(jnp.int32, (HALF, ROWS), 1) // MEM
    mask = key_at <= query_at
    late = 1 - flip
    for group in range(KV):
        key = split(keys, 0, group)
        value = split(keys, 1, group)
        d_key = []
        d_value = []
        for half in range(2):
            dq, dk, dv = pair(key[half], value[half], q_norm[group, half], grads_out[group, half],
                              lse2[group, half], delta[group, half], mask)
            d_query[group, half] = dq
            d_key.append(dk)
            d_value.append(dv)
        early_key = jnp.where(flipped, key[1], key[0])
        early_value = jnp.where(flipped, value[1], value[0])
        dq, dk, dv = pair(early_key, early_value, q_norm[group, late], grads_out[group, late],
                          lse2[group, late], delta[group, late])
        d_query[group, late] += dq
        for half in range(2):
            here = flipped if half == 1 else jnp.logical_not(flipped)
            rows = pl.ds(half * TOK + group, HALF, stride=KV)
            d_local[0, rows, :] = d_key[half] + jnp.where(here, dk, 0.0)
            d_local[1, rows, :] = d_value[half] + jnp.where(here, dv, 0.0)
    k_part[...] = jnp.sum(d_local[0] * k_unit, axis=0, keepdims=True)


def build_kernel(info, k_own, v_own, k_behind, v_behind, out):
    place = info[1]
    for slot in range(SLOTS):
        own = slot > place
        out[slot, 0:TOK * KV] = jnp.where(own, k_own[...], k_behind[...])
        out[slot, TOK * KV:PAYLOAD] = jnp.where(own, v_own[...], v_behind[...])


def three_terms(row):
    high = row.astype(BF16).astype(F32)
    rest = row - high
    middle = rest.astype(BF16).astype(F32)
    return [high, middle, rest - middle]


def main_kernel(info, blocks, q_norm, grads_out, lse2, delta, d_query0, q_raw, q_gain, k_gain, k_part,
                d_q_raw, pieces, d_query, units, keys, vals, grads):
    flip = info[0]
    flipped = flip == 1
    late = 1 - flip
    for slot in range(SLOTS):
        unit, _ = unit_of(blocks[slot, 0:TOK * KV].astype(F32))
        units[slot] = unit
        keys[slot] = (unit * k_gain[...]).astype(BF16).astype(F32)
        vals[slot] = blocks[slot, TOK * KV:PAYLOAD].astype(F32)
    d_query[...] = d_query0[...]
    for group in range(KV):
        early_keys, early_values, late_keys, late_values = [], [], [], []
        for slot in range(SLOTS):
            key = split(keys, slot, group)
            value = split(vals, slot, group)
            early_keys.append(jnp.where(flipped, key[1], key[0]))
            late_keys.append(jnp.where(flipped, key[0], key[1]))
            early_values.append(jnp.where(flipped, value[1], value[0]))
            late_values.append(jnp.where(flipped, value[0], value[1]))
        dq, dk_all, dv_all = pair(jnp.concatenate(early_keys, 0), jnp.concatenate(early_values, 0),
                                  q_norm[group, late], grads_out[group, late],
                                  lse2[group, late], delta[group, late])
        d_query[group, late] += dq
        for slot in range(SLOTS):
            wraps = info[2 + slot] == 1
            half = jnp.where(wraps, late, flip)
            dq, dk, dv = pair(jnp.where(wraps, late_keys[slot], early_keys[slot]),
                              jnp.where(wraps, late_values[slot], early_values[slot]),
                              q_norm[group, half], grads_out[group, half],
                              lse2[group, half], delta[group, half])
            d_query[group, half] += dq
            span = slice(slot * HALF, (slot + 1) * HALF)
            for which, everyone, rest in ((0, dk_all[span], dk), (1, dv_all[span], dv)):
                of_early = everyone + jnp.where(wraps, 0.0, rest)
                of_late = jnp.where(wraps, rest, 0.0)
                at = slot * 2 + which
                grads[at, pl.ds(group, HALF, stride=KV), :] = jnp.where(flipped, of_late, of_early)
                grads[at, pl.ds(TOK + group, HALF, stride=KV), :] = jnp.where(flipped, of_early, of_late)

    k_sum = k_part[...]
    for slot in range(SLOTS):
        k_sum += jnp.sum(grads[2 * slot] * units[slot], axis=0, keepdims=True)
        pieces[slot, 0:TOK * KV] = grads[2 * slot].astype(BF16)
        pieces[slot, TOK * KV:PAYLOAD] = grads[2 * slot + 1].astype(BF16)

    q_sum = jnp.zeros((1, DH), F32)
    gain = q_gain[...]
    for half in range(2):
        tokens = slice(half * HALF, (half + 1) * HALF)
        raw = q_raw[tokens].astype(F32)
        made = []
        for group in range(KV):
            rows = raw[:, group * MEM:(group + 1) * MEM, :].reshape(ROWS, DH)
            unit, inverse = unit_of(rows)
            gradient = d_query[group, half]
            q_sum += jnp.sum(gradient * unit, axis=0, keepdims=True)
            made.append(norm_backward(unit, inverse, gain, gradient).reshape(HALF, MEM, DH))
        d_q_raw[tokens] = jnp.concatenate(made, axis=1).astype(BF16)

    terms = three_terms(q_sum) + three_terms(k_sum) + [jnp.zeros((EXTRA - 6, DH), F32)]
    extra = jnp.concatenate(terms, axis=0).astype(BF16)
    for slot in range(SLOTS):
        pieces[slot, PAYLOAD:PAYLOAD + EXTRA] = extra


def sum_kernel(info, pieces, d_local, own, behind, gains):
    place = info[1]
    total = jnp.concatenate([d_local[0], d_local[1]], axis=0)
    others = jnp.zeros((PAYLOAD, DH), F32)
    extra = jnp.zeros((EXTRA, DH), F32)
    for slot in range(SLOTS):
        piece = pieces[slot, 0:PAYLOAD].astype(F32)
        ahead = slot > place
        total += jnp.where(ahead, piece, 0.0)
        others += jnp.where(ahead, 0.0, piece)
        extra += pieces[slot, PAYLOAD:PAYLOAD + EXTRA].astype(F32)
    own[...] = total
    behind[...] = others.astype(BF16)
    both = jnp.concatenate([jnp.sum(extra[0:3], axis=0, keepdims=True), jnp.sum(extra[3:6], axis=0, keepdims=True)], axis=0)
    for place in range(gains.shape[0]):
        gains[place] = both


def relay_kernel(gathered, spread):
    both = jnp.sum(gathered[...], axis=0)
    for place in range(spread.shape[0]):
        spread[place] = both


def last_kernel(own, arrived, k_raw, k_gain, gathered, d_k_raw, d_values, q_sum, k_sum):
    total = own[...] + arrived[...].astype(F32)
    unit, inverse = unit_of(k_raw[...].astype(F32))
    d_k_raw[...] = norm_backward(unit, inverse, k_gain[...], total[0:TOK * KV]).astype(BF16)
    d_values[...] = total[TOK * KV:PAYLOAD].astype(BF16)
    both = jnp.sum(gathered[...], axis=0)
    q_sum[...] = both[0:1]
    k_sum[...] = both[1:2]


def call(kernel, outs, specs, scratch=(), flops=0, size=0):
    return pl.pallas_call(
        kernel,
        out_shape=[jax.ShapeDtypeStruct(*o) for o in outs],
        in_specs=specs,
        out_specs=[VMEM] * len(outs),
        scratch_shapes=list(scratch),
        compiler_params=PARAMS,
        cost_estimate=pl.CostEstimate(flops=flops, bytes_accessed=size, transcendentals=0),
    )


def step(block, axes, distance):
    size = lax.axis_size(axes)
    return lax.ppermute(block, axes, [((i - distance) % size, i) for i in range(size)])


def per_device(q_raw, k_raw, values, attn_out, d_out, lse, q_gain, k_gain, span_order):
    k_own = k_raw.reshape(TOK * KV, DH)
    v_own = values.reshape(TOK * KV, DH)
    k_behind = step(k_own, ("zh", "y"), 1)
    v_behind = step(v_own, ("zh", "y"), 1)

    place = lax.axis_index("x")
    block = lax.axis_index(("zh", "y", "x"))
    spans = lax.dynamic_slice_in_dim(span_order, 2 * block, 2)
    flip = (spans[0] > spans[1]).astype(jnp.int32)
    early = jnp.minimum(spans[0], spans[1])
    hops = (place - jnp.arange(SLOTS, dtype=jnp.int32) - 1) % SLOTS + 1
    info = jnp.concatenate([jnp.stack([flip, place]), (hops > early).astype(jnp.int32)])
    q_gain = q_gain.reshape(1, DH)
    k_gain = k_gain.reshape(1, DH)
    lse2 = (lse * LOG2E).reshape(KV, MEM, TOK).transpose(0, 2, 1).reshape(KV, 2, 1, ROWS)

    q_norm, grads_out, delta, d_query0, d_local, k_part = call(
        prep_kernel,
        [((KV, 2, ROWS, DH), BF16), ((KV, 2, ROWS, DH), BF16), ((KV, 2, 1, ROWS), F32),
         ((KV, 2, ROWS, DH), F32), ((2, TOK * KV, DH), F32), ((1, DH), F32)],
        [SMEM] + [VMEM] * 8,
        [pltpu.VMEM((2, TOK * KV, DH), F32)],
        flops=int(6e9), size=1 << 22,
    )(info, q_raw, d_out, attn_out, lse2, k_own, v_own, q_gain, k_gain)

    (blocks,) = call(build_kernel, [((SLOTS, PAYLOAD, DH), BF16)], [SMEM] + [VMEM] * 4)(
        info, k_own, v_own, k_behind, v_behind)
    blocks = lax.all_to_all(blocks, "x", 0, 0)
    d_q_raw, pieces = call(
        main_kernel,
        [((TOK, KV * MEM, DH), BF16), ((SLOTS, PAYLOAD + EXTRA, DH), BF16)],
        [SMEM] + [VMEM] * 10,
        [pltpu.VMEM((KV, 2, ROWS, DH), F32), pltpu.VMEM((SLOTS, TOK * KV, DH), F32),
         pltpu.VMEM((SLOTS, TOK * KV, DH), F32), pltpu.VMEM((SLOTS, TOK * KV, DH), F32),
         pltpu.VMEM((2 * SLOTS, TOK * KV, DH), F32)],
    )(info, blocks, q_norm, grads_out, lse2, delta, d_query0, q_raw, q_gain, k_gain, k_part)
    pieces = lax.all_to_all(pieces, "x", 0, 0)
    own, behind, gains = call(
        sum_kernel,
        [((PAYLOAD, DH), F32), ((PAYLOAD, DH), BF16), ((lax.axis_size("y"), 2, DH), F32)],
        [SMEM] + [VMEM] * 2,
    )(info, pieces, d_local)
    arrived = step(behind, ("zh", "y"), -1)
    gains = lax.all_to_all(gains, "y", 0, 0)
    others = ("zh", "zl", "c")
    (gains,) = call(relay_kernel, [((lax.axis_size(others), 2, DH), F32)], [VMEM])(gains)
    gains = lax.all_to_all(gains, others, 0, 0)
    d_k_raw, d_values, d_q_gain, d_k_gain = call(
        last_kernel,
        [((TOK * KV, DH), BF16), ((TOK * KV, DH), BF16), ((1, DH), F32), ((1, DH), F32)],
        [VMEM] * 5,
    )(own, arrived, k_own, k_gain, gains)
    return (d_q_raw, d_k_raw.reshape(TOK, KV, DH), d_values.reshape(TOK, KV, DH),
            d_q_gain.reshape(DH), d_k_gain.reshape(DH))


def solution(mesh):
    devices = np.asarray(mesh.devices).reshape(4, 8, 4, 2, 2)
    mesh = jax.sharding.Mesh(devices, ("zh", "y", "x", "zl", "c"))
    rows = ("zh", "y", "x")
    heads = ("zl", "c")
    placed = P(rows, heads, None)
    return jax.shard_map(
        per_device,
        mesh=mesh,
        in_specs=(placed,) * 5 + (P(heads, rows), P(), P(), P()),
        out_specs=(placed,) * 3 + (P(), P()),
        check_vma=False,
    )
```

```python
import jax
import jax.numpy as jnp
import numpy as np
from jax import lax
from jax.experimental import pallas as pl
from jax.experimental.pallas import tpu as pltpu
from jax.sharding import PartitionSpec as P

F32 = jnp.float32
BF16 = jnp.bfloat16
EPSILON = 1e-06
TOK = 128
HALF = 64
KV = 2
MEM = 8
DH = 128
ROWS = HALF * MEM
SLOTS = 4
SCALE = DH ** (-0.5)
LOG2E = float(np.log2(np.e))
PAYLOAD = 2 * TOK * KV
EXTRA = 16
STATS = PAYLOAD + 8
FIRST = ("y",)
SECOND = ("zh", "zl", "c")
VMEM = pl.BlockSpec(memory_space=pltpu.VMEM)
SMEM = pl.BlockSpec(memory_space=pltpu.SMEM)
PARAMS = pltpu.CompilerParams(vmem_limit_bytes=12 * 1024 * 1024)


def facts(spans):
    block = (lax.axis_index("zh") * 8 + lax.axis_index("y")) * SLOTS + lax.axis_index("x")
    place = lax.axis_index("x")
    first, second = spans[2 * block], spans[2 * block + 1]
    flip = (first > second).astype(jnp.int32)
    early = jnp.minimum(first, second)
    wraps = [lax.rem(place - slot + SLOTS - 1, SLOTS) + 1 > early for slot in range(SLOTS)]
    return flip, place, wraps


def dot_nt(a, b):
    return lax.dot_general(a, b, (((1,), (1,)), ((), ())), preferred_element_type=F32)


def dot_nn(a, b):
    return lax.dot_general(a, b, (((1,), (0,)), ((), ())), preferred_element_type=F32)


def dot_tn(a, b):
    return lax.dot_general(a, b, (((0,), (0,)), ((), ())), preferred_element_type=F32)


def unit_of(floats):
    inverse = lax.rsqrt(jnp.mean(floats * floats, axis=-1, keepdims=True) + EPSILON)
    return floats * inverse, inverse


def norm_backward(unit, inverse, gain, gradient):
    scaled = gradient * gain
    projected = jnp.mean(scaled * unit, axis=-1, keepdims=True)
    return (scaled - unit * projected) * inverse


def pair(key, value, query, grad_out, lse2, delta, mask=None, keep=None):
    scores = dot_nt(key, query)
    probs = jnp.exp2(scores * (SCALE * LOG2E) - lse2)
    if mask is not None:
        probs = jnp.where(mask, probs, 0.0)
    if keep is not None:
        probs = jnp.concatenate([jnp.where(flag, probs[slot * HALF:(slot + 1) * HALF], 0.0)
                                 for slot, flag in enumerate(keep)], axis=0)
    d_probs = dot_nt(value, grad_out)
    d_scores = (probs * (d_probs - delta)).astype(BF16)
    d_value = dot_nn(probs.astype(BF16), grad_out)
    d_key = dot_nn(d_scores, query) * SCALE
    d_query = dot_tn(d_scores, key) * SCALE
    return d_query, d_key, d_value


def split(scratch, at, group):
    first = scratch[at, pl.ds(group, HALF, stride=KV), :].astype(BF16)
    second = scratch[at, pl.ds(TOK + group, HALF, stride=KV), :].astype(BF16)
    return first, second


def prep_kernel(spans, q_raw, d_out, attn_out, lse2, k_raw, values, q_gain, k_gain,
                q_norm, grads_out, d_query, d_local, keys, made, stats):
    flip, _, wrapped = facts(spans)
    flipped = flip == 1
    gain = q_gain[...].reshape(1, DH)
    ones = jnp.ones((8, DH), F32)
    for group in range(KV):
        q_rows = q_raw[...].astype(F32)[:, group * MEM:(group + 1) * MEM, :]
        unit, _ = unit_of(q_rows.reshape(TOK * MEM, DH))
        normed = (unit * gain).astype(BF16)
        grads = d_out[...].astype(F32)[:, group * MEM:(group + 1) * MEM, :].reshape(TOK * MEM, DH)
        outs = attn_out[...].astype(F32)[:, group * MEM:(group + 1) * MEM, :].reshape(TOK * MEM, DH)
        row_delta = lax.dot_general(ones, grads * outs, (((1,), (1,)), ((), ())),
                                    precision=lax.Precision.HIGHEST, preferred_element_type=F32)
        grads = grads.astype(BF16)
        for half in range(2):
            rows = slice(half * ROWS, (half + 1) * ROWS)
            q_norm[group, half] = normed[rows]
            grads_out[group, half] = grads[rows]
            stats[group, half, 0:1] = lse2[group, half]
            stats[group, half, 1:2] = row_delta[0:1, rows]

    k_unit, _ = unit_of(k_raw[...].astype(F32))
    keys[0] = (k_unit * k_gain[...].reshape(1, DH)).astype(BF16).astype(F32)
    keys[1] = values[...].astype(F32)
    key_at = lax.broadcasted_iota(jnp.int32, (HALF, ROWS), 0)
    query_at = lax.broadcasted_iota(jnp.int32, (HALF, ROWS), 1) // MEM
    mask = key_at <= query_at
    late = 1 - flip
    for group in range(KV):
        key = split(keys, 0, group)
        value = split(keys, 1, group)
        d_key = []
        d_value = []
        for half in range(2):
            dq, dk, dv = pair(key[half], value[half], q_norm[group, half], grads_out[group, half],
                              stats[group, half, 0:1], stats[group, half, 1:2], mask)
            d_query[group, half] = dq
            d_key.append(dk)
            d_value.append(dv)
        early_key = jnp.where(flipped, key[1], key[0])
        early_value = jnp.where(flipped, value[1], value[0])
        dq, dk, dv = pair(early_key, early_value, q_norm[group, late], grads_out[group, late],
                          stats[group, late, 0:1], stats[group, late, 1:2])
        d_query[group, late] += dq
        for half in range(2):
            here = flipped if half == 1 else jnp.logical_not(flipped)
            rows = pl.ds(half * TOK + group, HALF, stride=KV)
            made[0, rows, :] = d_key[half] + jnp.where(here, dk, 0.0)
            made[1, rows, :] = d_value[half] + jnp.where(here, dv, 0.0)
    for group in range(KV):
        for half in range(2):
            base = STATS + (group * 2 + half) * 8
            for part in range(4):
                lanes = slice(part * DH, (part + 1) * DH)
                d_local[base + part:base + part + 1] = stats[group, half, 0:1, lanes]
                d_local[base + 4 + part:base + 5 + part] = stats[group, half, 1:2, lanes]
    d_local[0:TOK * KV] = made[0]
    d_local[TOK * KV:PAYLOAD] = made[1]
    flags = [jnp.full((1, DH), flag, jnp.int32).astype(F32) for flag in [flip] + [w.astype(jnp.int32) for w in wrapped]]
    d_local[PAYLOAD:PAYLOAD + 8] = jnp.concatenate(
        [jnp.sum(made[0] * k_unit, axis=0, keepdims=True), gain, k_gain[...].reshape(1, DH)] + flags, axis=0)


def build_kernel(k_own, v_own, k_behind, v_behind, out):
    place = lax.axis_index("x")
    for slot in range(SLOTS):
        own = slot > place
        out[slot, 0:TOK * KV] = jnp.where(own, k_own[...], k_behind[...])
        out[slot, TOK * KV:PAYLOAD] = jnp.where(own, v_own[...], v_behind[...])


def three_terms(row):
    high = row.astype(BF16).astype(F32)
    rest = row - high
    middle = rest.astype(BF16).astype(F32)
    return [high, middle, rest - middle]


def main_kernel(blocks, q_norm, grads_out, d_query0, q_raw, d_local,
                d_q_raw, pieces, d_query, units, keys, vals, grads, sums):
    q_gain, k_gain = d_local[PAYLOAD + 1:PAYLOAD + 2], d_local[PAYLOAD + 2:PAYLOAD + 3]
    flags = [jnp.max(d_local[PAYLOAD + at:PAYLOAD + at + 1]).astype(jnp.int32) for at in range(3, 8)]
    flip, wrapped = flags[0], [flag == 1 for flag in flags[1:]]
    flipped = flip == 1
    late = 1 - flip
    inside = [jnp.logical_not(flag) for flag in wrapped]
    some_inside = inside[0] | inside[1] | inside[2] | inside[3]
    some_wrapped = wrapped[0] | wrapped[1] | wrapped[2] | wrapped[3]
    for slot in range(SLOTS):
        unit, _ = unit_of(blocks[slot, 0:TOK * KV].astype(F32))
        units[slot] = unit
        keys[slot] = (unit * k_gain).astype(BF16).astype(F32)
        vals[slot] = blocks[slot, TOK * KV:PAYLOAD].astype(F32)

    def stats(group, half):
        rows = d_local[pl.ds(pl.multiple_of(STATS + (group * 2 + half) * 8, 8), 8), :]
        return [jnp.concatenate([rows[at + part:at + part + 1] for part in range(4)], axis=1) for at in (0, 4)]

    d_query[...] = d_query0[...]
    for group in range(KV):
        def gather(scratch, want_late):
            halves = [split(scratch, slot, group) for slot in range(SLOTS)]
            first = flipped if want_late else jnp.logical_not(flipped)
            return jnp.concatenate([jnp.where(first, half[0], half[1]) for half in halves], axis=0)

        early_keys, early_values = gather(keys, False), gather(vals, False)
        dq, dk, dv = pair(early_keys, early_values, q_norm[group, late], grads_out[group, late],
                          *stats(group, late))
        d_query[group, late] += dq
        sums[0] = dk
        sums[1] = dv
        sums[2] = jnp.zeros_like(dk)
        sums[3] = jnp.zeros_like(dv)

        @pl.when(some_inside)
        def _():
            dq, dk, dv = pair(early_keys, early_values, q_norm[group, flip], grads_out[group, flip],
                              *stats(group, flip), keep=inside)
            d_query[group, flip] += dq
            sums[0] += dk
            sums[1] += dv

        @pl.when(some_wrapped)
        def _():
            dq, dk, dv = pair(gather(keys, True), gather(vals, True), q_norm[group, late], grads_out[group, late],
                              *stats(group, late), keep=wrapped)
            d_query[group, late] += dq
            sums[2] = dk
            sums[3] = dv

        for slot in range(SLOTS):
            span = slice(slot * HALF, (slot + 1) * HALF)
            for which in range(2):
                of_early, of_late = sums[which, span], sums[2 + which, span]
                at = slot * 2 + which
                grads[at, pl.ds(group, HALF, stride=KV), :] = jnp.where(flipped, of_late, of_early)
                grads[at, pl.ds(TOK + group, HALF, stride=KV), :] = jnp.where(flipped, of_early, of_late)

    k_sum = d_local[PAYLOAD:PAYLOAD + 1]
    for slot in range(SLOTS):
        k_sum += jnp.sum(grads[2 * slot] * units[slot], axis=0, keepdims=True)
        pieces[slot, 0:TOK * KV] = grads[2 * slot].astype(BF16)
        pieces[slot, TOK * KV:PAYLOAD] = grads[2 * slot + 1].astype(BF16)

    q_sum = jnp.zeros((1, DH), F32)
    gain = q_gain
    for half in range(2):
        tokens = slice(half * HALF, (half + 1) * HALF)
        raw = q_raw[tokens].astype(F32)
        made = []
        for group in range(KV):
            rows = raw[:, group * MEM:(group + 1) * MEM, :].reshape(ROWS, DH)
            unit, inverse = unit_of(rows)
            gradient = d_query[group, half]
            q_sum += jnp.sum(gradient * unit, axis=0, keepdims=True)
            made.append(norm_backward(unit, inverse, gain, gradient).reshape(HALF, MEM, DH))
        d_q_raw[tokens] = jnp.concatenate(made, axis=1).astype(BF16)

    terms = three_terms(q_sum) + three_terms(k_sum) + [jnp.zeros((EXTRA - 6, DH), F32)]
    extra = jnp.concatenate(terms, axis=0).astype(BF16)
    for slot in range(SLOTS):
        pieces[slot, PAYLOAD:PAYLOAD + EXTRA] = extra


def sum_kernel(pieces, d_local, own, behind, gains):
    place = lax.axis_index("x")
    total = d_local[0:PAYLOAD]
    others = jnp.zeros((PAYLOAD, DH), F32)
    extra = jnp.zeros((EXTRA, DH), F32)
    for slot in range(SLOTS):
        piece = pieces[slot, 0:PAYLOAD].astype(F32)
        ahead = slot > place
        total += jnp.where(ahead, piece, 0.0)
        others += jnp.where(ahead, 0.0, piece)
        extra += pieces[slot, PAYLOAD:PAYLOAD + EXTRA].astype(F32)
    own[...] = total
    behind[...] = others.astype(BF16)
    both = jnp.concatenate([jnp.sum(extra[0:3], axis=0, keepdims=True), jnp.sum(extra[3:6], axis=0, keepdims=True)], axis=0)
    for peer in range(gains.shape[0]):
        gains[peer] = both


def relay_kernel(gathered, spread):
    both = jnp.sum(gathered[...], axis=0)
    for peer in range(spread.shape[0]):
        spread[peer] = both


def last_kernel(own, arrived, k_raw, k_gain, gathered, d_k_raw, d_values, q_sum, k_sum):
    total = own[...] + arrived[...].astype(F32)
    unit, inverse = unit_of(k_raw[...].astype(F32))
    d_k_raw[...] = norm_backward(unit, inverse, k_gain[...].reshape(1, DH), total[0:TOK * KV]).astype(BF16)
    d_values[...] = total[TOK * KV:PAYLOAD].astype(BF16)
    both = jnp.sum(gathered[...], axis=0)
    q_sum[...] = both[0]
    k_sum[...] = both[1]


def call(kernel, outs, specs, scratch=(), flops=0, size=0):
    return pl.pallas_call(
        kernel,
        out_shape=[jax.ShapeDtypeStruct(*o) for o in outs],
        in_specs=specs,
        out_specs=[VMEM] * len(outs),
        scratch_shapes=list(scratch),
        compiler_params=PARAMS,
        cost_estimate=pl.CostEstimate(flops=flops, bytes_accessed=size, transcendentals=0),
    )


def step(block, axes, distance):
    size = lax.axis_size(axes)
    return lax.ppermute(block, axes, [((i - distance) % size, i) for i in range(size)])


def per_device(q_raw, k_raw, values, attn_out, d_out, lse, q_gain, k_gain, span_order):
    k_own = k_raw.reshape(TOK * KV, DH)
    v_own = values.reshape(TOK * KV, DH)
    k_behind = step(k_own, ("zh", "y"), 1)
    v_behind = step(v_own, ("zh", "y"), 1)

    lse2 = (lse * LOG2E).reshape(KV, MEM, TOK).transpose(0, 2, 1).reshape(KV, 2, 1, ROWS)

    q_norm, grads_out, d_query0, d_local = call(
        prep_kernel,
        [((KV, 2, ROWS, DH), BF16), ((KV, 2, ROWS, DH), BF16),
         ((KV, 2, ROWS, DH), F32), ((STATS + KV * 2 * 8, DH), F32)],
        [SMEM] + [VMEM] * 8,
        [pltpu.VMEM((2, TOK * KV, DH), F32)] * 2 + [pltpu.VMEM((KV, 2, 8, ROWS), F32)],
        flops=int(6e9), size=1 << 22,
    )(span_order, q_raw, d_out, attn_out, lse2, k_own, v_own, q_gain, k_gain)

    (blocks,) = call(build_kernel, [((SLOTS, PAYLOAD, DH), BF16)], [VMEM] * 4)(
        k_own, v_own, k_behind, v_behind)
    blocks = lax.all_to_all(blocks, "x", 0, 0)
    d_q_raw, pieces = call(
        main_kernel,
        [((TOK, KV * MEM, DH), BF16), ((SLOTS, PAYLOAD + EXTRA, DH), BF16)],
        [VMEM] * 6,
        [pltpu.VMEM((KV, 2, ROWS, DH), F32)] + [pltpu.VMEM((SLOTS, TOK * KV, DH), F32)] * 3
        + [pltpu.VMEM((2 * SLOTS, TOK * KV, DH), F32), pltpu.VMEM((4, SLOTS * HALF, DH), F32)],
    )(blocks, q_norm, grads_out, d_query0, q_raw, d_local)
    pieces = lax.all_to_all(pieces, "x", 0, 0)
    own, behind, gains = call(
        sum_kernel,
        [((PAYLOAD, DH), F32), ((PAYLOAD, DH), BF16), ((lax.axis_size(FIRST), 2, DH), F32)],
        [VMEM] * 2,
    )(pieces, d_local)
    arrived = step(behind, ("zh", "y"), -1)
    gains = lax.all_to_all(gains, FIRST, 0, 0)
    (gains,) = call(relay_kernel, [((lax.axis_size(SECOND), 2, DH), F32)], [VMEM])(gains)
    gains = lax.all_to_all(gains, SECOND, 0, 0)
    d_k_raw, d_values, d_q_gain, d_k_gain = call(
        last_kernel,
        [((TOK * KV, DH), BF16), ((TOK * KV, DH), BF16), ((DH,), F32), ((DH,), F32)],
        [VMEM] * 5,
    )(own, arrived, k_own, k_gain, gains)
    return (d_q_raw, d_k_raw.reshape(TOK, KV, DH), d_values.reshape(TOK, KV, DH),
            d_q_gain, d_k_gain)


def solution(mesh):
    devices = np.asarray(mesh.devices).reshape(4, 8, 4, 2, 2)
    mesh = jax.sharding.Mesh(devices, ("zh", "y", "x", "zl", "c"))
    rows = ("zh", "y", "x")
    heads = ("zl", "c")
    placed = P(rows, heads, None)
    return jax.shard_map(
        per_device,
        mesh=mesh,
        in_specs=(placed,) * 5 + (P(heads, rows), P(), P(), P()),
        out_specs=(placed,) * 3 + (P(), P()),
        check_vma=False,
    )
```

```python
import jax
import jax.numpy as jnp
import numpy as np
from jax import lax
from jax.experimental import pallas as pl
from jax.experimental.pallas import tpu as pltpu
from jax.sharding import PartitionSpec as P

F32 = jnp.float32
BF16 = jnp.bfloat16
EPSILON = 1e-06
TOK = 128
HALF = 64
KV = 2
MEM = 8
DH = 128
ROWS = HALF * MEM
SLOTS = 4
SCALE = DH ** (-0.5)
LOG2E = float(np.log2(np.e))
PAYLOAD = 2 * TOK * KV
EXTRA = 16
BUILD_SIZE = 1 << 20
STATS = PAYLOAD + 8
FIRST = ("zh", "zl", "c")
SECOND = ("y",)
ANY = pl.BlockSpec(memory_space=pl.ANY)
VMEM = pl.BlockSpec(memory_space=pltpu.VMEM)
SMEM = pl.BlockSpec(memory_space=pltpu.SMEM)
PARAMS = pltpu.CompilerParams(vmem_limit_bytes=12 * 1024 * 1024)


def facts(spans):
    block = (lax.axis_index("zh") * 8 + lax.axis_index("y")) * SLOTS + lax.axis_index("x")
    place = lax.axis_index("x")
    first, second = spans[2 * block], spans[2 * block + 1]
    flip = (first > second).astype(jnp.int32)
    early = jnp.minimum(first, second)
    wraps = [lax.rem(place - slot + SLOTS - 1, SLOTS) + 1 > early for slot in range(SLOTS)]
    return flip, place, wraps


def dot_nt(a, b):
    return lax.dot_general(a, b, (((1,), (1,)), ((), ())), preferred_element_type=F32)


def dot_nn(a, b):
    return lax.dot_general(a, b, (((1,), (0,)), ((), ())), preferred_element_type=F32)


def dot_tn(a, b):
    return lax.dot_general(a, b, (((0,), (0,)), ((), ())), preferred_element_type=F32)


def unit_of(floats):
    inverse = lax.rsqrt(jnp.mean(floats * floats, axis=-1, keepdims=True) + EPSILON)
    return floats * inverse, inverse


def norm_backward(unit, inverse, gain, gradient):
    scaled = gradient * gain
    projected = jnp.mean(scaled * unit, axis=-1, keepdims=True)
    return (scaled - unit * projected) * inverse


def pair(key, value, query, grad_out, lse2, delta, mask=None, keep=None):
    scores = dot_nt(key, query)
    probs = jnp.exp2(scores * (SCALE * LOG2E) - lse2)
    if mask is not None:
        probs = jnp.where(mask, probs, 0.0)
    if keep is not None:
        probs = jnp.concatenate([jnp.where(flag, probs[slot * HALF:(slot + 1) * HALF], 0.0)
                                 for slot, flag in enumerate(keep)], axis=0)
    d_probs = dot_nt(value, grad_out)
    d_scores = (probs * (d_probs - delta)).astype(BF16)
    d_value = dot_nn(probs.astype(BF16), grad_out)
    d_key = dot_nn(d_scores, query) * SCALE
    d_query = dot_tn(d_scores, key) * SCALE
    return d_query, d_key, d_value


def split(scratch, at, group):
    first = scratch[at, pl.ds(group, HALF, stride=KV), :].astype(BF16)
    second = scratch[at, pl.ds(TOK + group, HALF, stride=KV), :].astype(BF16)
    return first, second


def prep_kernel(spans, q_raw, d_out, attn_out, lse2, k_raw, values, q_gain, k_gain,
                q_norm, grads_out, d_query, d_local, keys, made, stats):
    flip, _, wrapped = facts(spans)
    flipped = flip == 1
    gain = q_gain[...].reshape(1, DH)
    ones = jnp.ones((8, DH), F32)
    for group in range(KV):
        q_rows = q_raw[...].astype(F32)[:, group * MEM:(group + 1) * MEM, :]
        unit, _ = unit_of(q_rows.reshape(TOK * MEM, DH))
        normed = (unit * gain).astype(BF16)
        grads = d_out[...].astype(F32)[:, group * MEM:(group + 1) * MEM, :].reshape(TOK * MEM, DH)
        outs = attn_out[...].astype(F32)[:, group * MEM:(group + 1) * MEM, :].reshape(TOK * MEM, DH)
        row_delta = lax.dot_general(ones, grads * outs, (((1,), (1,)), ((), ())),
                                    precision=lax.Precision.HIGHEST, preferred_element_type=F32)
        grads = grads.astype(BF16)
        for half in range(2):
            rows = slice(half * ROWS, (half + 1) * ROWS)
            q_norm[group, half] = normed[rows]
            grads_out[group, half] = grads[rows]
            stats[group, half, 0:1] = lse2[group, half]
            stats[group, half, 1:2] = row_delta[0:1, rows]

    k_unit, _ = unit_of(k_raw[...].astype(F32))
    keys[0] = (k_unit * k_gain[...].reshape(1, DH)).astype(BF16).astype(F32)
    keys[1] = values[...].astype(F32)
    key_at = lax.broadcasted_iota(jnp.int32, (HALF, ROWS), 0)
    query_at = lax.broadcasted_iota(jnp.int32, (HALF, ROWS), 1) // MEM
    mask = key_at <= query_at
    late = 1 - flip
    for group in range(KV):
        key = split(keys, 0, group)
        value = split(keys, 1, group)
        d_key = []
        d_value = []
        for half in range(2):
            dq, dk, dv = pair(key[half], value[half], q_norm[group, half], grads_out[group, half],
                              stats[group, half, 0:1], stats[group, half, 1:2], mask)
            d_query[group, half] = dq
            d_key.append(dk)
            d_value.append(dv)
        early_key = jnp.where(flipped, key[1], key[0])
        early_value = jnp.where(flipped, value[1], value[0])
        dq, dk, dv = pair(early_key, early_value, q_norm[group, late], grads_out[group, late],
                          stats[group, late, 0:1], stats[group, late, 1:2])
        d_query[group, late] += dq
        for half in range(2):
            here = flipped if half == 1 else jnp.logical_not(flipped)
            rows = pl.ds(half * TOK + group, HALF, stride=KV)
            made[0, rows, :] = d_key[half] + jnp.where(here, dk, 0.0)
            made[1, rows, :] = d_value[half] + jnp.where(here, dv, 0.0)
    for group in range(KV):
        for half in range(2):
            base = STATS + (group * 2 + half) * 8
            for part in range(4):
                lanes = slice(part * DH, (part + 1) * DH)
                d_local[base + part:base + part + 1] = stats[group, half, 0:1, lanes]
                d_local[base + 4 + part:base + 5 + part] = stats[group, half, 1:2, lanes]
    d_local[0:TOK * KV] = made[0]
    d_local[TOK * KV:PAYLOAD] = made[1]
    flags = [jnp.full((1, DH), flag, jnp.int32).astype(F32) for flag in [flip] + [w.astype(jnp.int32) for w in wrapped]]
    d_local[PAYLOAD:PAYLOAD + 8] = jnp.concatenate(
        [jnp.sum(made[0] * k_unit, axis=0, keepdims=True), gain, k_gain[...].reshape(1, DH)] + flags, axis=0)


def build_kernel(k_own, v_own, k_behind, v_behind, out, sems):
    place = lax.axis_index("x")
    for slot in range(SLOTS):
        for which, (own, behind) in enumerate(((k_own, k_behind), (v_own, v_behind))):
            target = out.at[slot, pl.ds(which * TOK * KV, TOK * KV)]

            @pl.when(slot > place)
            def _():
                pltpu.make_async_copy(own, target, sems.at[slot, which]).start()

            @pl.when(slot <= place)
            def _():
                pltpu.make_async_copy(behind, target, sems.at[slot, which]).start()

    for slot in range(SLOTS):
        for which in range(2):
            target = out.at[slot, pl.ds(which * TOK * KV, TOK * KV)]
            pltpu.make_async_copy(k_behind, target, sems.at[slot, which]).wait()


def three_terms(row):
    high = row.astype(BF16).astype(F32)
    rest = row - high
    middle = rest.astype(BF16).astype(F32)
    return [high, middle, rest - middle]


def main_kernel(blocks, q_norm, grads_out, d_query0, q_raw, d_local,
                d_q_raw, pieces, d_query, units, keys, vals, grads, sums, d_q_rows, sems):
    q_gain, k_gain = d_local[PAYLOAD + 1:PAYLOAD + 2], d_local[PAYLOAD + 2:PAYLOAD + 3]
    flags = [jnp.max(d_local[PAYLOAD + at:PAYLOAD + at + 1]).astype(jnp.int32) for at in range(3, 8)]
    flip, wrapped = flags[0], [flag == 1 for flag in flags[1:]]
    flipped = flip == 1
    late = 1 - flip
    inside = [jnp.logical_not(flag) for flag in wrapped]
    some_inside = inside[0] | inside[1] | inside[2] | inside[3]
    some_wrapped = wrapped[0] | wrapped[1] | wrapped[2] | wrapped[3]
    for slot in range(SLOTS):
        unit, _ = unit_of(blocks[slot, 0:TOK * KV].astype(F32))
        units[slot] = unit
        keys[slot] = (unit * k_gain).astype(BF16).astype(F32)
        vals[slot] = blocks[slot, TOK * KV:PAYLOAD].astype(F32)

    def stats(group, half):
        rows = d_local[pl.ds(pl.multiple_of(STATS + (group * 2 + half) * 8, 8), 8), :]
        return [jnp.concatenate([rows[at + part:at + part + 1] for part in range(4)], axis=1) for at in (0, 4)]

    early_keys, early_values = [], []

    def gather(scratch, group, want_late):
        halves = [split(scratch, slot, group) for slot in range(SLOTS)]
        first = flipped if want_late else jnp.logical_not(flipped)
        return jnp.concatenate([jnp.where(first, half[0], half[1]) for half in halves], axis=0)

    def finish(half, q_sum):
        raw = q_raw[pl.ds(pl.multiple_of(half * HALF, HALF), HALF)].astype(F32)
        made = []
        for group in range(KV):
            unit, inverse = unit_of(raw[:, group * MEM:(group + 1) * MEM, :].reshape(ROWS, DH))
            gradient = d_query[group, half]
            q_sum += jnp.sum(gradient * unit, axis=0, keepdims=True)
            made.append(norm_backward(unit, inverse, q_gain, gradient).reshape(HALF, MEM, DH))
        tokens = pl.ds(pl.multiple_of(half * HALF, HALF), HALF)
        d_q_rows[tokens] = jnp.concatenate(made, axis=1).astype(BF16)
        return q_sum, tokens

    for group in range(KV):
        early_keys.append(gather(keys, group, False))
        early_values.append(gather(vals, group, False))
        d_query[group, flip] = d_query0[group, flip]
        for at in range(4):
            sums[group, at] = jnp.zeros((SLOTS * HALF, DH), F32)

        @pl.when(some_inside)
        def _():
            dq, dk, dv = pair(early_keys[group], early_values[group], q_norm[group, flip], grads_out[group, flip],
                              *stats(group, flip), keep=inside)
            d_query[group, flip] += dq
            sums[group, 0] = dk
            sums[group, 1] = dv

    q_sum, tokens = finish(flip, jnp.zeros((1, DH), F32))
    early_copy = pltpu.make_async_copy(d_q_rows.at[tokens], d_q_raw.at[tokens], sems.at[0])
    early_copy.start()
    for group in range(KV):
        dq, dk, dv = pair(early_keys[group], early_values[group], q_norm[group, late], grads_out[group, late],
                          *stats(group, late))
        d_query[group, late] = d_query0[group, late] + dq
        sums[group, 0] += dk
        sums[group, 1] += dv

        @pl.when(some_wrapped)
        def _():
            dq, dk, dv = pair(gather(keys, group, True), gather(vals, group, True), q_norm[group, late],
                              grads_out[group, late], *stats(group, late), keep=wrapped)
            d_query[group, late] += dq
            sums[group, 2] = dk
            sums[group, 3] = dv

    q_sum, tokens = finish(late, q_sum)
    late_copy = pltpu.make_async_copy(d_q_rows.at[tokens], d_q_raw.at[tokens], sems.at[1])
    late_copy.start()
    for group in range(KV):
        for slot in range(SLOTS):
            span = slice(slot * HALF, (slot + 1) * HALF)
            for which in range(2):
                of_early, of_late = sums[group, which, span], sums[group, 2 + which, span]
                at = slot * 2 + which
                grads[at, pl.ds(group, HALF, stride=KV), :] = jnp.where(flipped, of_late, of_early)
                grads[at, pl.ds(TOK + group, HALF, stride=KV), :] = jnp.where(flipped, of_early, of_late)

    k_sum = d_local[PAYLOAD:PAYLOAD + 1]
    for slot in range(SLOTS):
        k_sum += jnp.sum(grads[2 * slot] * units[slot], axis=0, keepdims=True)
        pieces[slot, 0:TOK * KV] = grads[2 * slot].astype(BF16)
        pieces[slot, TOK * KV:PAYLOAD] = grads[2 * slot + 1].astype(BF16)

    terms = three_terms(q_sum) + three_terms(k_sum) + [jnp.zeros((EXTRA - 6, DH), F32)]
    extra = jnp.concatenate(terms, axis=0).astype(BF16)
    for slot in range(SLOTS):
        pieces[slot, PAYLOAD:PAYLOAD + EXTRA] = extra
    early_copy.wait()
    late_copy.wait()


def sum_kernel(pieces, d_local, own, behind, gains):
    place = lax.axis_index("x")
    total = d_local[0:PAYLOAD]
    others = jnp.zeros((PAYLOAD, DH), F32)
    extra = jnp.zeros((EXTRA, DH), F32)
    for slot in range(SLOTS):
        piece = pieces[slot, 0:PAYLOAD].astype(F32)
        ahead = slot > place
        total += jnp.where(ahead, piece, 0.0)
        others += jnp.where(ahead, 0.0, piece)
        extra += pieces[slot, PAYLOAD:PAYLOAD + EXTRA].astype(F32)
    own[...] = total
    behind[...] = others.astype(BF16)
    both = jnp.concatenate([jnp.sum(extra[0:3], axis=0, keepdims=True), jnp.sum(extra[3:6], axis=0, keepdims=True)], axis=0)
    for peer in range(gains.shape[0]):
        gains[peer] = both


def relay_kernel(gathered, spread):
    both = jnp.sum(gathered[...], axis=0)
    for peer in range(spread.shape[0]):
        spread[peer] = both


def last_kernel(own, arrived, k_raw, k_gain, gathered, d_k_raw, d_values, q_sum, k_sum):
    total = own[...] + arrived[...].astype(F32)
    unit, inverse = unit_of(k_raw[...].astype(F32))
    d_k_raw[...] = norm_backward(unit, inverse, k_gain[...].reshape(1, DH), total[0:TOK * KV]).astype(BF16)
    d_values[...] = total[TOK * KV:PAYLOAD].astype(BF16)
    both = jnp.sum(gathered[...], axis=0)
    q_sum[...] = both[0]
    k_sum[...] = both[1]


def call(kernel, outs, specs, scratch=(), flops=0, size=0, out_specs=None):
    return pl.pallas_call(
        kernel,
        out_shape=[jax.ShapeDtypeStruct(*o) for o in outs],
        in_specs=specs,
        out_specs=out_specs or [VMEM] * len(outs),
        scratch_shapes=list(scratch),
        compiler_params=PARAMS,
        cost_estimate=pl.CostEstimate(flops=flops, bytes_accessed=size, transcendentals=0),
    )


def step(block, axes, distance):
    size = lax.axis_size(axes)
    return lax.ppermute(block, axes, [((i - distance) % size, i) for i in range(size)])


def per_device(q_raw, k_raw, values, attn_out, d_out, lse, q_gain, k_gain, span_order):
    k_own = k_raw.reshape(TOK * KV, DH)
    v_own = values.reshape(TOK * KV, DH)
    k_behind = step(k_own, ("zh", "y"), 1)
    v_behind = step(v_own, ("zh", "y"), 1)

    lse2 = (lse * LOG2E).reshape(KV, MEM, TOK).transpose(0, 2, 1).reshape(KV, 2, 1, ROWS)

    q_norm, grads_out, d_query0, d_local = call(
        prep_kernel,
        [((KV, 2, ROWS, DH), BF16), ((KV, 2, ROWS, DH), BF16),
         ((KV, 2, ROWS, DH), F32), ((STATS + KV * 2 * 8, DH), F32)],
        [SMEM] + [VMEM] * 8,
        [pltpu.VMEM((2, TOK * KV, DH), F32)] * 2 + [pltpu.VMEM((KV, 2, 8, ROWS), F32)],
        flops=int(6e9), size=1 << 22,
    )(span_order, q_raw, d_out, attn_out, lse2, k_own, v_own, q_gain, k_gain)

    (blocks,) = call(build_kernel, [((SLOTS, PAYLOAD, DH), BF16)], [VMEM] * 4, [pltpu.SemaphoreType.DMA((SLOTS, 2))],
                     size=BUILD_SIZE, out_specs=[ANY])(k_own, v_own, k_behind, v_behind)
    blocks = lax.all_to_all(blocks, "x", 0, 0)
    d_q_raw, pieces = call(
        main_kernel,
        [((TOK, KV * MEM, DH), BF16), ((SLOTS, PAYLOAD + EXTRA, DH), BF16)],
        [VMEM] * 6,
        [pltpu.VMEM((KV, 2, ROWS, DH), F32)] + [pltpu.VMEM((SLOTS, TOK * KV, DH), F32)] * 3
        + [pltpu.VMEM((2 * SLOTS, TOK * KV, DH), F32), pltpu.VMEM((KV, 4, SLOTS * HALF, DH), F32),
           pltpu.VMEM((TOK, KV * MEM, DH), BF16), pltpu.SemaphoreType.DMA((2,))],
        out_specs=[ANY, VMEM],
    )(blocks, q_norm, grads_out, d_query0, q_raw, d_local)
    pieces = lax.all_to_all(pieces, "x", 0, 0)
    own, behind, gains = call(
        sum_kernel,
        [((PAYLOAD, DH), F32), ((PAYLOAD, DH), BF16), ((lax.axis_size(FIRST), 2, DH), F32)],
        [VMEM] * 2,
    )(pieces, d_local)
    arrived = step(behind, ("zh", "y"), -1)
    gains = lax.all_to_all(gains, FIRST, 0, 0)
    (gains,) = call(relay_kernel, [((lax.axis_size(SECOND), 2, DH), F32)], [VMEM])(gains)
    gains = lax.all_to_all(gains, SECOND, 0, 0)
    d_k_raw, d_values, d_q_gain, d_k_gain = call(
        last_kernel,
        [((TOK * KV, DH), BF16), ((TOK * KV, DH), BF16), ((DH,), F32), ((DH,), F32)],
        [VMEM] * 5,
    )(own, arrived, k_own, k_gain, gains)
    return (d_q_raw, d_k_raw.reshape(TOK, KV, DH), d_values.reshape(TOK, KV, DH),
            d_q_gain, d_k_gain)


def solution(mesh):
    devices = np.asarray(mesh.devices).reshape(4, 8, 4, 2, 2)
    mesh = jax.sharding.Mesh(devices, ("zh", "y", "x", "zl", "c"))
    rows = ("zh", "y", "x")
    heads = ("zl", "c")
    placed = P(rows, heads, None)
    return jax.shard_map(
        per_device,
        mesh=mesh,
        in_specs=(placed,) * 5 + (P(heads, rows), P(), P(), P()),
        out_specs=(placed,) * 3 + (P(), P()),
        check_vma=False,
    )
```

```python
import jax
import jax.numpy as jnp
import numpy as np
from jax import lax
from jax.experimental import pallas as pl
from jax.experimental.pallas import tpu as pltpu
from jax.sharding import PartitionSpec as P

F32 = jnp.float32
BF16 = jnp.bfloat16
EPSILON = 1e-06
TOK = 128
HALF = 64
KV = 2
MEM = 8
DH = 128
ROWS = HALF * MEM
SLOTS = 4
SCALE = DH ** (-0.5)
LOG2E = float(np.log2(np.e))
PAYLOAD = 2 * TOK * KV
EXTRA = 16
BUILD_SIZE = 1 << 20
STATS = PAYLOAD + 8
FIRST = ("zh", "zl", "c")
SECOND = ("y",)
ANY = pl.BlockSpec(memory_space=pl.ANY)
VMEM = pl.BlockSpec(memory_space=pltpu.VMEM)
SMEM = pl.BlockSpec(memory_space=pltpu.SMEM)
PARAMS = pltpu.CompilerParams(vmem_limit_bytes=12 * 1024 * 1024)


def facts(spans):
    block = (lax.axis_index("zh") * 8 + lax.axis_index("y")) * SLOTS + lax.axis_index("x")
    place = lax.axis_index("x")
    first, second = spans[2 * block], spans[2 * block + 1]
    flip = (first > second).astype(jnp.int32)
    early = jnp.minimum(first, second)
    wraps = [lax.rem(place - slot + SLOTS - 1, SLOTS) + 1 > early for slot in range(SLOTS)]
    return flip, place, wraps


def dot_nt(a, b):
    return lax.dot_general(a, b, (((1,), (1,)), ((), ())), preferred_element_type=F32)


def dot_nn(a, b):
    return lax.dot_general(a, b, (((1,), (0,)), ((), ())), preferred_element_type=F32)


def dot_tn(a, b):
    return lax.dot_general(a, b, (((0,), (0,)), ((), ())), preferred_element_type=F32)


def unit_of(floats):
    inverse = lax.rsqrt(jnp.mean(floats * floats, axis=-1, keepdims=True) + EPSILON)
    return floats * inverse, inverse


def norm_backward(unit, inverse, gain, gradient):
    scaled = gradient * gain
    projected = jnp.mean(scaled * unit, axis=-1, keepdims=True)
    return (scaled - unit * projected) * inverse


def pair(key, value, query, grad_out, lse2, delta, mask=None, keep=None):
    scores = dot_nt(key, query)
    probs = jnp.exp2(scores * (SCALE * LOG2E) - lse2)
    if mask is not None:
        probs = jnp.where(mask, probs, 0.0)
    if keep is not None:
        probs = jnp.concatenate([jnp.where(flag, probs[slot * HALF:(slot + 1) * HALF], 0.0)
                                 for slot, flag in enumerate(keep)], axis=0)
    d_probs = dot_nt(value, grad_out)
    d_scores = (probs * (d_probs - delta)).astype(BF16)
    d_value = dot_nn(probs.astype(BF16), grad_out)
    d_key = dot_nn(d_scores, query) * SCALE
    d_query = dot_tn(d_scores, key) * SCALE
    return d_query, d_key, d_value


def split(scratch, at, group):
    first = scratch[at, pl.ds(group, HALF, stride=KV), :].astype(BF16)
    second = scratch[at, pl.ds(TOK + group, HALF, stride=KV), :].astype(BF16)
    return first, second


def prep_kernel(spans, q_raw, d_out, attn_out, lse2, k_raw, values, q_gain, k_gain,
                q_norm, grads_out, d_query, d_local, keys, made, stats):
    flip, _, wrapped = facts(spans)
    flipped = flip == 1
    gain = q_gain[...].reshape(1, DH)
    ones = jnp.ones((8, DH), BF16)
    for group in range(KV):
        q_rows = q_raw[...].astype(F32)[:, group * MEM:(group + 1) * MEM, :]
        unit, _ = unit_of(q_rows.reshape(TOK * MEM, DH))
        normed = (unit * gain).astype(BF16)
        grads = d_out[...].astype(F32)[:, group * MEM:(group + 1) * MEM, :].reshape(TOK * MEM, DH)
        outs = attn_out[...].astype(F32)[:, group * MEM:(group + 1) * MEM, :].reshape(TOK * MEM, DH)
        row_delta = sum(dot_nt(ones, term.astype(BF16)) for term in three_terms(grads * outs))
        grads = grads.astype(BF16)
        for half in range(2):
            rows = slice(half * ROWS, (half + 1) * ROWS)
            q_norm[group, half] = normed[rows]
            grads_out[group, half] = grads[rows]
            stats[group, half, 0:1] = lse2[group, half]
            stats[group, half, 1:2] = row_delta[0:1, rows]

    k_unit, _ = unit_of(k_raw[...].astype(F32))
    keys[0] = (k_unit * k_gain[...].reshape(1, DH)).astype(BF16).astype(F32)
    keys[1] = values[...].astype(F32)
    key_at = lax.broadcasted_iota(jnp.int32, (HALF, ROWS), 0)
    query_at = lax.broadcasted_iota(jnp.int32, (HALF, ROWS), 1) // MEM
    mask = key_at <= query_at
    late = 1 - flip
    for group in range(KV):
        key = split(keys, 0, group)
        value = split(keys, 1, group)
        d_key = []
        d_value = []
        for half in range(2):
            dq, dk, dv = pair(key[half], value[half], q_norm[group, half], grads_out[group, half],
                              stats[group, half, 0:1], stats[group, half, 1:2], mask)
            d_query[group, half] = dq
            d_key.append(dk)
            d_value.append(dv)
        early_key = jnp.where(flipped, key[1], key[0])
        early_value = jnp.where(flipped, value[1], value[0])
        dq, dk, dv = pair(early_key, early_value, q_norm[group, late], grads_out[group, late],
                          stats[group, late, 0:1], stats[group, late, 1:2])
        d_query[group, late] += dq
        for half in range(2):
            here = flipped if half == 1 else jnp.logical_not(flipped)
            rows = pl.ds(half * TOK + group, HALF, stride=KV)
            made[0, rows, :] = d_key[half] + jnp.where(here, dk, 0.0)
            made[1, rows, :] = d_value[half] + jnp.where(here, dv, 0.0)
    for group in range(KV):
        for half in range(2):
            base = STATS + (group * 2 + half) * 8
            for part in range(4):
                lanes = slice(part * DH, (part + 1) * DH)
                d_local[base + part:base + part + 1] = stats[group, half, 0:1, lanes]
                d_local[base + 4 + part:base + 5 + part] = stats[group, half, 1:2, lanes]
    d_local[0:TOK * KV] = made[0]
    d_local[TOK * KV:PAYLOAD] = made[1]
    flags = [jnp.full((1, DH), flag, jnp.int32).astype(F32) for flag in [flip] + [w.astype(jnp.int32) for w in wrapped]]
    d_local[PAYLOAD:PAYLOAD + 8] = jnp.concatenate(
        [jnp.sum(made[0] * k_unit, axis=0, keepdims=True), gain, k_gain[...].reshape(1, DH)] + flags, axis=0)


def build_kernel(k_own, v_own, k_behind, v_behind, out, sems):
    place = lax.axis_index("x")
    for slot in range(SLOTS):
        for which, (own, behind) in enumerate(((k_own, k_behind), (v_own, v_behind))):
            target = out.at[slot, pl.ds(which * TOK * KV, TOK * KV)]

            @pl.when(slot > place)
            def _():
                pltpu.make_async_copy(own, target, sems.at[slot, which]).start()

            @pl.when(slot <= place)
            def _():
                pltpu.make_async_copy(behind, target, sems.at[slot, which]).start()

    for slot in range(SLOTS):
        for which in range(2):
            target = out.at[slot, pl.ds(which * TOK * KV, TOK * KV)]
            pltpu.make_async_copy(k_behind, target, sems.at[slot, which]).wait()


def three_terms(floats):
    high = floats.astype(BF16).astype(F32)
    rest = floats - high
    middle = rest.astype(BF16).astype(F32)
    return [high, middle, rest - middle]


def main_kernel(blocks, q_norm, grads_out, d_query0, q_raw, d_local,
                d_q_raw, pieces, d_query, units, keys, vals, grads, sums, d_q_rows, sems):
    q_gain, k_gain = d_local[PAYLOAD + 1:PAYLOAD + 2], d_local[PAYLOAD + 2:PAYLOAD + 3]
    flags = [jnp.max(d_local[PAYLOAD + at:PAYLOAD + at + 1]).astype(jnp.int32) for at in range(3, 8)]
    flip, wrapped = flags[0], [flag == 1 for flag in flags[1:]]
    flipped = flip == 1
    late = 1 - flip
    inside = [jnp.logical_not(flag) for flag in wrapped]
    some_inside = inside[0] | inside[1] | inside[2] | inside[3]
    some_wrapped = wrapped[0] | wrapped[1] | wrapped[2] | wrapped[3]
    for slot in range(SLOTS):
        unit, _ = unit_of(blocks[slot, 0:TOK * KV].astype(F32))
        units[slot] = unit
        keys[slot] = (unit * k_gain).astype(BF16).astype(F32)
        vals[slot] = blocks[slot, TOK * KV:PAYLOAD].astype(F32)

    def stats(group, half):
        rows = d_local[pl.ds(pl.multiple_of(STATS + (group * 2 + half) * 8, 8), 8), :]
        return [jnp.concatenate([rows[at + part:at + part + 1] for part in range(4)], axis=1) for at in (0, 4)]

    early_keys, early_values = [], []

    def gather(scratch, group, want_late):
        halves = [split(scratch, slot, group) for slot in range(SLOTS)]
        first = flipped if want_late else jnp.logical_not(flipped)
        return jnp.concatenate([jnp.where(first, half[0], half[1]) for half in halves], axis=0)

    def finish(half, q_sum):
        raw = q_raw[pl.ds(pl.multiple_of(half * HALF, HALF), HALF)].astype(F32)
        made = []
        for group in range(KV):
            unit, inverse = unit_of(raw[:, group * MEM:(group + 1) * MEM, :].reshape(ROWS, DH))
            gradient = d_query[group, half]
            q_sum += jnp.sum(gradient * unit, axis=0, keepdims=True)
            made.append(norm_backward(unit, inverse, q_gain, gradient).reshape(HALF, MEM, DH))
        tokens = pl.ds(pl.multiple_of(half * HALF, HALF), HALF)
        d_q_rows[tokens] = jnp.concatenate(made, axis=1).astype(BF16)
        return q_sum, tokens

    for group in range(KV):
        early_keys.append(gather(keys, group, False))
        early_values.append(gather(vals, group, False))
        d_query[group, flip] = d_query0[group, flip]
        for at in range(4):
            sums[group, at] = jnp.zeros((SLOTS * HALF, DH), F32)

        @pl.when(some_inside)
        def _():
            dq, dk, dv = pair(early_keys[group], early_values[group], q_norm[group, flip], grads_out[group, flip],
                              *stats(group, flip), keep=inside)
            d_query[group, flip] += dq
            sums[group, 0] = dk
            sums[group, 1] = dv

    q_sum, tokens = finish(flip, jnp.zeros((1, DH), F32))
    early_copy = pltpu.make_async_copy(d_q_rows.at[tokens], d_q_raw.at[tokens], sems.at[0])
    early_copy.start()
    for group in range(KV):
        dq, dk, dv = pair(early_keys[group], early_values[group], q_norm[group, late], grads_out[group, late],
                          *stats(group, late))
        d_query[group, late] = d_query0[group, late] + dq
        sums[group, 0] += dk
        sums[group, 1] += dv

        @pl.when(some_wrapped)
        def _():
            dq, dk, dv = pair(gather(keys, group, True), gather(vals, group, True), q_norm[group, late],
                              grads_out[group, late], *stats(group, late), keep=wrapped)
            d_query[group, late] += dq
            sums[group, 2] = dk
            sums[group, 3] = dv

    q_sum, tokens = finish(late, q_sum)
    late_copy = pltpu.make_async_copy(d_q_rows.at[tokens], d_q_raw.at[tokens], sems.at[1])
    late_copy.start()
    for group in range(KV):
        for slot in range(SLOTS):
            span = slice(slot * HALF, (slot + 1) * HALF)
            for which in range(2):
                of_early, of_late = sums[group, which, span], sums[group, 2 + which, span]
                at = slot * 2 + which
                grads[at, pl.ds(group, HALF, stride=KV), :] = jnp.where(flipped, of_late, of_early)
                grads[at, pl.ds(TOK + group, HALF, stride=KV), :] = jnp.where(flipped, of_early, of_late)

    k_sum = d_local[PAYLOAD:PAYLOAD + 1]
    for slot in range(SLOTS):
        k_sum += jnp.sum(grads[2 * slot] * units[slot], axis=0, keepdims=True)
        pieces[slot, 0:TOK * KV] = grads[2 * slot].astype(BF16)
        pieces[slot, TOK * KV:PAYLOAD] = grads[2 * slot + 1].astype(BF16)

    terms = three_terms(q_sum) + three_terms(k_sum) + [jnp.zeros((EXTRA - 6, DH), F32)]
    extra = jnp.concatenate(terms, axis=0).astype(BF16)
    for slot in range(SLOTS):
        pieces[slot, PAYLOAD:PAYLOAD + EXTRA] = extra
    early_copy.wait()
    late_copy.wait()


def sum_kernel(pieces, d_local, own, behind, gains):
    place = lax.axis_index("x")
    total = d_local[0:PAYLOAD]
    others = jnp.zeros((PAYLOAD, DH), F32)
    extra = jnp.zeros((EXTRA, DH), F32)
    for slot in range(SLOTS):
        piece = pieces[slot, 0:PAYLOAD].astype(F32)
        ahead = slot > place
        total += jnp.where(ahead, piece, 0.0)
        others += jnp.where(ahead, 0.0, piece)
        extra += pieces[slot, PAYLOAD:PAYLOAD + EXTRA].astype(F32)
    own[...] = total
    behind[...] = others.astype(BF16)
    both = jnp.concatenate([jnp.sum(extra[0:3], axis=0, keepdims=True), jnp.sum(extra[3:6], axis=0, keepdims=True)], axis=0)
    for peer in range(gains.shape[0]):
        gains[peer] = both


def relay_kernel(gathered, spread):
    both = jnp.sum(gathered[...], axis=0)
    for peer in range(spread.shape[0]):
        spread[peer] = both


def last_kernel(own, arrived, k_raw, k_gain, gathered, d_k_raw, d_values, q_sum, k_sum):
    total = own[...] + arrived[...].astype(F32)
    unit, inverse = unit_of(k_raw[...].astype(F32))
    d_k_raw[...] = norm_backward(unit, inverse, k_gain[...].reshape(1, DH), total[0:TOK * KV]).astype(BF16)
    d_values[...] = total[TOK * KV:PAYLOAD].astype(BF16)
    both = jnp.sum(gathered[...], axis=0)
    q_sum[...] = both[0]
    k_sum[...] = both[1]


def call(kernel, outs, specs, scratch=(), flops=0, size=0, out_specs=None):
    return pl.pallas_call(
        kernel,
        out_shape=[jax.ShapeDtypeStruct(*o) for o in outs],
        in_specs=specs,
        out_specs=out_specs or [VMEM] * len(outs),
        scratch_shapes=list(scratch),
        compiler_params=PARAMS,
        cost_estimate=pl.CostEstimate(flops=flops, bytes_accessed=size, transcendentals=0),
    )


def step(block, axes, distance):
    size = lax.axis_size(axes)
    return lax.ppermute(block, axes, [((i - distance) % size, i) for i in range(size)])


def per_device(q_raw, k_raw, values, attn_out, d_out, lse, q_gain, k_gain, span_order):
    k_own = k_raw.reshape(TOK * KV, DH)
    v_own = values.reshape(TOK * KV, DH)
    k_behind = step(k_own, ("zh", "y"), 1)
    v_behind = step(v_own, ("zh", "y"), 1)

    lse2 = (lse * LOG2E).reshape(KV, MEM, TOK).transpose(0, 2, 1).reshape(KV, 2, 1, ROWS)

    q_norm, grads_out, d_query0, d_local = call(
        prep_kernel,
        [((KV, 2, ROWS, DH), BF16), ((KV, 2, ROWS, DH), BF16),
         ((KV, 2, ROWS, DH), F32), ((STATS + KV * 2 * 8, DH), F32)],
        [SMEM] + [VMEM] * 8,
        [pltpu.VMEM((2, TOK * KV, DH), F32)] * 2 + [pltpu.VMEM((KV, 2, 8, ROWS), F32)],
        flops=int(6e9), size=1 << 22,
    )(span_order, q_raw, d_out, attn_out, lse2, k_own, v_own, q_gain, k_gain)

    (blocks,) = call(build_kernel, [((SLOTS, PAYLOAD, DH), BF16)], [VMEM] * 4, [pltpu.SemaphoreType.DMA((SLOTS, 2))],
                     size=BUILD_SIZE, out_specs=[ANY])(k_own, v_own, k_behind, v_behind)
    blocks = lax.all_to_all(blocks, "x", 0, 0)
    d_q_raw, pieces = call(
        main_kernel,
        [((TOK, KV * MEM, DH), BF16), ((SLOTS, PAYLOAD + EXTRA, DH), BF16)],
        [VMEM] * 6,
        [pltpu.VMEM((KV, 2, ROWS, DH), F32)] + [pltpu.VMEM((SLOTS, TOK * KV, DH), F32)] * 3
        + [pltpu.VMEM((2 * SLOTS, TOK * KV, DH), F32), pltpu.VMEM((KV, 4, SLOTS * HALF, DH), F32),
           pltpu.VMEM((TOK, KV * MEM, DH), BF16), pltpu.SemaphoreType.DMA((2,))],
        out_specs=[ANY, VMEM],
    )(blocks, q_norm, grads_out, d_query0, q_raw, d_local)
    pieces = lax.all_to_all(pieces, "x", 0, 0)
    own, behind, gains = call(
        sum_kernel,
        [((PAYLOAD, DH), F32), ((PAYLOAD, DH), BF16), ((lax.axis_size(FIRST), 2, DH), F32)],
        [VMEM] * 2,
    )(pieces, d_local)
    arrived = step(behind, ("zh", "y"), -1)
    gains = lax.all_to_all(gains, FIRST, 0, 0)
    (gains,) = call(relay_kernel, [((lax.axis_size(SECOND), 2, DH), F32)], [VMEM])(gains)
    gains = lax.all_to_all(gains, SECOND, 0, 0)
    d_k_raw, d_values, d_q_gain, d_k_gain = call(
        last_kernel,
        [((TOK * KV, DH), BF16), ((TOK * KV, DH), BF16), ((DH,), F32), ((DH,), F32)],
        [VMEM] * 5,
    )(own, arrived, k_own, k_gain, gains)
    return (d_q_raw, d_k_raw.reshape(TOK, KV, DH), d_values.reshape(TOK, KV, DH),
            d_q_gain, d_k_gain)


def solution(mesh):
    devices = np.asarray(mesh.devices).reshape(4, 8, 4, 2, 2)
    mesh = jax.sharding.Mesh(devices, ("zh", "y", "x", "zl", "c"))
    rows = ("zh", "y", "x")
    heads = ("zl", "c")
    placed = P(rows, heads, None)
    return jax.shard_map(
        per_device,
        mesh=mesh,
        in_specs=(placed,) * 5 + (P(heads, rows), P(), P(), P()),
        out_specs=(placed,) * 3 + (P(), P()),
        check_vma=False,
    )
```

```python
import jax
import jax.numpy as jnp
import numpy as np
from jax import lax
from jax.experimental import pallas as pl
from jax.experimental.pallas import tpu as pltpu
from jax.sharding import PartitionSpec as P

F32 = jnp.float32
BF16 = jnp.bfloat16
EPSILON = 1e-06
TOK = 128
HALF = 64
KV = 2
MEM = 8
DH = 128
ROWS = HALF * MEM
SLOTS = 4
SCALE = DH ** (-0.5)
LOG2E = float(np.log2(np.e))
PAYLOAD = 2 * TOK * KV
EXTRA = 16
BUILD_SIZE = 1 << 20
STATS = PAYLOAD + 8
FIRST = ("zh", "zl", "c")
SECOND = ("y",)
ANY = pl.BlockSpec(memory_space=pl.ANY)
VMEM = pl.BlockSpec(memory_space=pltpu.VMEM)
SMEM = pl.BlockSpec(memory_space=pltpu.SMEM)
PARAMS = pltpu.CompilerParams(vmem_limit_bytes=12 * 1024 * 1024)


def facts(spans):
    block = (lax.axis_index("zh") * 8 + lax.axis_index("y")) * SLOTS + lax.axis_index("x")
    place = lax.axis_index("x")
    first, second = spans[2 * block], spans[2 * block + 1]
    flip = (first > second).astype(jnp.int32)
    early = jnp.minimum(first, second)
    wraps = [lax.rem(place - slot + SLOTS - 1, SLOTS) + 1 > early for slot in range(SLOTS)]
    return flip, place, wraps


def dot_nt(a, b):
    return lax.dot_general(a, b, (((1,), (1,)), ((), ())), preferred_element_type=F32)


def dot_nn(a, b):
    return lax.dot_general(a, b, (((1,), (0,)), ((), ())), preferred_element_type=F32)


def dot_tn(a, b):
    return lax.dot_general(a, b, (((0,), (0,)), ((), ())), preferred_element_type=F32)


def unit_of(floats):
    inverse = lax.rsqrt(jnp.mean(floats * floats, axis=-1, keepdims=True) + EPSILON)
    return floats * inverse, inverse


def norm_backward(unit, inverse, gain, gradient):
    scaled = gradient * gain
    projected = jnp.mean(scaled * unit, axis=-1, keepdims=True)
    return (scaled - unit * projected) * inverse


def pair(key, value, query, grad_out, lse2, delta, mask=None, keep=None):
    scores = dot_nt(key, query)
    probs = jnp.exp2(scores * (SCALE * LOG2E) - lse2)
    if mask is not None:
        probs = jnp.where(mask, probs, 0.0)
    if keep is not None:
        probs = jnp.concatenate([jnp.where(flag, probs[slot * HALF:(slot + 1) * HALF], 0.0)
                                 for slot, flag in enumerate(keep)], axis=0)
    d_probs = dot_nt(value, grad_out)
    d_scores = (probs * (d_probs - delta)).astype(BF16)
    d_value = dot_nn(probs.astype(BF16), grad_out)
    d_key = dot_nn(d_scores, query) * SCALE
    d_query = dot_tn(d_scores, key) * SCALE
    return d_query, d_key, d_value


def split(scratch, at, group):
    first = scratch[at, pl.ds(group, HALF, stride=KV), :].astype(BF16)
    second = scratch[at, pl.ds(TOK + group, HALF, stride=KV), :].astype(BF16)
    return first, second


def prep_kernel(spans, q_raw, d_out, attn_out, lse2, k_raw, values, q_gain, k_gain,
                q_norm, grads_out, d_query, d_local, keys, made, stats):
    flip, _, wrapped = facts(spans)
    flipped = flip == 1
    gain = q_gain[...].reshape(1, DH)
    ones = jnp.ones((8, DH), BF16)
    for group in range(KV):
        q_rows = q_raw[...].astype(F32)[:, group * MEM:(group + 1) * MEM, :]
        unit, _ = unit_of(q_rows.reshape(TOK * MEM, DH))
        normed = (unit * gain).astype(BF16)
        grads = d_out[...].astype(F32)[:, group * MEM:(group + 1) * MEM, :].reshape(TOK * MEM, DH)
        outs = attn_out[...].astype(F32)[:, group * MEM:(group + 1) * MEM, :].reshape(TOK * MEM, DH)
        row_delta = sum(dot_nt(ones, term.astype(BF16)) for term in three_terms(grads * outs))
        grads = grads.astype(BF16)
        for half in range(2):
            rows = slice(half * ROWS, (half + 1) * ROWS)
            q_norm[group, half] = normed[rows]
            grads_out[group, half] = grads[rows]
            stats[group, half, 0:1] = lse2[group, half]
            stats[group, half, 1:2] = row_delta[0:1, rows]

    k_unit, _ = unit_of(k_raw[...].astype(F32))
    keys[0] = (k_unit * k_gain[...].reshape(1, DH)).astype(BF16).astype(F32)
    keys[1] = values[...].astype(F32)
    key_at = lax.broadcasted_iota(jnp.int32, (HALF, ROWS), 0)
    query_at = lax.broadcasted_iota(jnp.int32, (HALF, ROWS), 1) // MEM
    mask = key_at <= query_at
    late = 1 - flip
    for group in range(KV):
        key = split(keys, 0, group)
        value = split(keys, 1, group)
        d_key = []
        d_value = []
        for half in range(2):
            dq, dk, dv = pair(key[half], value[half], q_norm[group, half], grads_out[group, half],
                              stats[group, half, 0:1], stats[group, half, 1:2], mask)
            d_query[group, half] = dq
            d_key.append(dk)
            d_value.append(dv)
        early_key = jnp.where(flipped, key[1], key[0])
        early_value = jnp.where(flipped, value[1], value[0])
        dq, dk, dv = pair(early_key, early_value, q_norm[group, late], grads_out[group, late],
                          stats[group, late, 0:1], stats[group, late, 1:2])
        d_query[group, late] += dq
        for half in range(2):
            here = flipped if half == 1 else jnp.logical_not(flipped)
            rows = pl.ds(half * TOK + group, HALF, stride=KV)
            made[0, rows, :] = d_key[half] + jnp.where(here, dk, 0.0)
            made[1, rows, :] = d_value[half] + jnp.where(here, dv, 0.0)
    for group in range(KV):
        for half in range(2):
            base = STATS + (group * 2 + half) * 8
            for part in range(4):
                lanes = slice(part * DH, (part + 1) * DH)
                d_local[base + part:base + part + 1] = stats[group, half, 0:1, lanes]
                d_local[base + 4 + part:base + 5 + part] = stats[group, half, 1:2, lanes]
    d_local[0:TOK * KV] = made[0]
    d_local[TOK * KV:PAYLOAD] = made[1]
    flags = [jnp.full((1, DH), flag, jnp.int32).astype(F32) for flag in [flip] + [w.astype(jnp.int32) for w in wrapped]]
    d_local[PAYLOAD:PAYLOAD + 8] = jnp.concatenate(
        [jnp.sum(made[0] * k_unit, axis=0, keepdims=True), gain, k_gain[...].reshape(1, DH)] + flags, axis=0)


def three_terms(floats):
    high = floats.astype(BF16).astype(F32)
    rest = floats - high
    middle = rest.astype(BF16).astype(F32)
    return [high, middle, rest - middle]


def main_kernel(blocks, q_norm, grads_out, d_query0, q_raw, d_local,
                d_q_raw, pieces, d_query, units, keys, vals, grads, sums, d_q_rows, sems):
    q_gain, k_gain = d_local[PAYLOAD + 1:PAYLOAD + 2], d_local[PAYLOAD + 2:PAYLOAD + 3]
    flags = [jnp.max(d_local[PAYLOAD + at:PAYLOAD + at + 1]).astype(jnp.int32) for at in range(3, 8)]
    flip, wrapped = flags[0], [flag == 1 for flag in flags[1:]]
    flipped = flip == 1
    late = 1 - flip
    inside = [jnp.logical_not(flag) for flag in wrapped]
    some_inside = inside[0] | inside[1] | inside[2] | inside[3]
    some_wrapped = wrapped[0] | wrapped[1] | wrapped[2] | wrapped[3]
    for slot in range(SLOTS):
        unit, _ = unit_of(blocks[slot, 0:TOK * KV].astype(F32))
        units[slot] = unit
        keys[slot] = (unit * k_gain).astype(BF16).astype(F32)
        vals[slot] = blocks[slot, TOK * KV:PAYLOAD].astype(F32)

    def stats(group, half):
        rows = d_local[pl.ds(pl.multiple_of(STATS + (group * 2 + half) * 8, 8), 8), :]
        return [jnp.concatenate([rows[at + part:at + part + 1] for part in range(4)], axis=1) for at in (0, 4)]

    early_keys, early_values = [], []

    def gather(scratch, group, want_late):
        halves = [split(scratch, slot, group) for slot in range(SLOTS)]
        first = flipped if want_late else jnp.logical_not(flipped)
        return jnp.concatenate([jnp.where(first, half[0], half[1]) for half in halves], axis=0)

    def finish(half, q_sum):
        raw = q_raw[pl.ds(pl.multiple_of(half * HALF, HALF), HALF)].astype(F32)
        made = []
        for group in range(KV):
            unit, inverse = unit_of(raw[:, group * MEM:(group + 1) * MEM, :].reshape(ROWS, DH))
            gradient = d_query[group, half]
            q_sum += jnp.sum(gradient * unit, axis=0, keepdims=True)
            made.append(norm_backward(unit, inverse, q_gain, gradient).reshape(HALF, MEM, DH))
        tokens = pl.ds(pl.multiple_of(half * HALF, HALF), HALF)
        d_q_rows[tokens] = jnp.concatenate(made, axis=1).astype(BF16)
        return q_sum, tokens

    for group in range(KV):
        early_keys.append(gather(keys, group, False))
        early_values.append(gather(vals, group, False))
        d_query[group, flip] = d_query0[group, flip]
        for at in range(4):
            sums[group, at] = jnp.zeros((SLOTS * HALF, DH), F32)

        @pl.when(some_inside)
        def _():
            dq, dk, dv = pair(early_keys[group], early_values[group], q_norm[group, flip], grads_out[group, flip],
                              *stats(group, flip), keep=inside)
            d_query[group, flip] += dq
            sums[group, 0] = dk
            sums[group, 1] = dv

    def leave(half):
        copies = []
        for part in range(4):
            tokens = pl.ds(pl.multiple_of(half * HALF + part * 16, 16), 16)
            copies.append(pltpu.make_async_copy(d_q_rows.at[tokens], d_q_raw.at[tokens], sems.at[half, part]))
            copies[-1].start()
        return copies

    q_sum, _ = finish(flip, jnp.zeros((1, DH), F32))
    copies = leave(flip)
    for group in range(KV):
        dq, dk, dv = pair(early_keys[group], early_values[group], q_norm[group, late], grads_out[group, late],
                          *stats(group, late))
        d_query[group, late] = d_query0[group, late] + dq
        sums[group, 0] += dk
        sums[group, 1] += dv

        @pl.when(some_wrapped)
        def _():
            dq, dk, dv = pair(gather(keys, group, True), gather(vals, group, True), q_norm[group, late],
                              grads_out[group, late], *stats(group, late), keep=wrapped)
            d_query[group, late] += dq
            sums[group, 2] = dk
            sums[group, 3] = dv

    q_sum, _ = finish(late, q_sum)
    copies += leave(late)
    for group in range(KV):
        for slot in range(SLOTS):
            span = slice(slot * HALF, (slot + 1) * HALF)
            for which in range(2):
                of_early, of_late = sums[group, which, span], sums[group, 2 + which, span]
                at = slot * 2 + which
                grads[at, pl.ds(group, HALF, stride=KV), :] = jnp.where(flipped, of_late, of_early)
                grads[at, pl.ds(TOK + group, HALF, stride=KV), :] = jnp.where(flipped, of_early, of_late)

    k_sum = d_local[PAYLOAD:PAYLOAD + 1]
    for slot in range(SLOTS):
        k_sum += jnp.sum(grads[2 * slot] * units[slot], axis=0, keepdims=True)
        pieces[slot, 0:TOK * KV] = grads[2 * slot].astype(BF16)
        pieces[slot, TOK * KV:PAYLOAD] = grads[2 * slot + 1].astype(BF16)

    terms = three_terms(q_sum) + three_terms(k_sum) + [jnp.zeros((EXTRA - 6, DH), F32)]
    extra = jnp.concatenate(terms, axis=0).astype(BF16)
    for slot in range(SLOTS):
        pieces[slot, PAYLOAD:PAYLOAD + EXTRA] = extra
    for copy in copies:
        copy.wait()


def sum_kernel(pieces, d_local, own, behind, gains):
    place = lax.axis_index("x")
    total = d_local[0:PAYLOAD]
    others = jnp.zeros((PAYLOAD, DH), F32)
    extra = jnp.zeros((EXTRA, DH), F32)
    for slot in range(SLOTS):
        piece = pieces[slot, 0:PAYLOAD].astype(F32)
        ahead = slot > place
        total += jnp.where(ahead, piece, 0.0)
        others += jnp.where(ahead, 0.0, piece)
        extra += pieces[slot, PAYLOAD:PAYLOAD + EXTRA].astype(F32)
    own[...] = total
    behind[...] = others.astype(BF16)
    both = jnp.concatenate([jnp.sum(extra[0:3], axis=0, keepdims=True), jnp.sum(extra[3:6], axis=0, keepdims=True)], axis=0)
    for peer in range(gains.shape[0]):
        gains[peer] = both


def relay_kernel(gathered, spread):
    both = jnp.sum(gathered[...], axis=0)
    for peer in range(spread.shape[0]):
        spread[peer] = both


def last_kernel(own, arrived, k_raw, k_gain, gathered, d_k_raw, d_values, q_sum, k_sum):
    total = own[...] + arrived[...].astype(F32)
    unit, inverse = unit_of(k_raw[...].astype(F32))
    d_k_raw[...] = norm_backward(unit, inverse, k_gain[...].reshape(1, DH), total[0:TOK * KV]).astype(BF16)
    d_values[...] = total[TOK * KV:PAYLOAD].astype(BF16)
    both = jnp.sum(gathered[...], axis=0)
    q_sum[...] = both[0]
    k_sum[...] = both[1]


def call(kernel, outs, specs, scratch=(), flops=0, size=0, out_specs=None):
    return pl.pallas_call(
        kernel,
        out_shape=[jax.ShapeDtypeStruct(*o) for o in outs],
        in_specs=specs,
        out_specs=out_specs or [VMEM] * len(outs),
        scratch_shapes=list(scratch),
        compiler_params=PARAMS,
        cost_estimate=pl.CostEstimate(flops=flops, bytes_accessed=size, transcendentals=0),
    )


def step(block, axes, distance):
    size = lax.axis_size(axes)
    return lax.ppermute(block, axes, [((i - distance) % size, i) for i in range(size)])


def per_device(q_raw, k_raw, values, attn_out, d_out, lse, q_gain, k_gain, span_order):
    k_own = k_raw.reshape(TOK * KV, DH)
    v_own = values.reshape(TOK * KV, DH)
    k_behind = step(k_own, ("zh", "y"), 1)
    v_behind = step(v_own, ("zh", "y"), 1)

    lse2 = (lse * LOG2E).reshape(KV, MEM, TOK).transpose(0, 2, 1).reshape(KV, 2, 1, ROWS)

    q_norm, grads_out, d_query0, d_local = call(
        prep_kernel,
        [((KV, 2, ROWS, DH), BF16), ((KV, 2, ROWS, DH), BF16),
         ((KV, 2, ROWS, DH), F32), ((STATS + KV * 2 * 8, DH), F32)],
        [SMEM] + [VMEM] * 8,
        [pltpu.VMEM((2, TOK * KV, DH), F32)] * 2 + [pltpu.VMEM((KV, 2, 8, ROWS), F32)],
        flops=int(6e9), size=1 << 22,
    )(span_order, q_raw, d_out, attn_out, lse2, k_own, v_own, q_gain, k_gain)

    slot = lax.broadcasted_iota(jnp.int32, (SLOTS, PAYLOAD, DH), 0)
    own = jnp.concatenate([k_own, v_own], axis=0)[None]
    behind = jnp.concatenate([k_behind, v_behind], axis=0)[None]
    blocks = jnp.where(slot > lax.axis_index("x"), own, behind)
    blocks = lax.all_to_all(blocks, "x", 0, 0)
    d_q_raw, pieces = call(
        main_kernel,
        [((TOK, KV * MEM, DH), BF16), ((SLOTS, PAYLOAD + EXTRA, DH), BF16)],
        [VMEM] * 6,
        [pltpu.VMEM((KV, 2, ROWS, DH), F32)] + [pltpu.VMEM((SLOTS, TOK * KV, DH), F32)] * 3
        + [pltpu.VMEM((2 * SLOTS, TOK * KV, DH), F32), pltpu.VMEM((KV, 4, SLOTS * HALF, DH), F32),
           pltpu.VMEM((TOK, KV * MEM, DH), BF16), pltpu.SemaphoreType.DMA((2, 4))],
        out_specs=[ANY, VMEM],
    )(blocks, q_norm, grads_out, d_query0, q_raw, d_local)
    pieces = lax.all_to_all(pieces, "x", 0, 0)
    own, behind, gains = call(
        sum_kernel,
        [((PAYLOAD, DH), F32), ((PAYLOAD, DH), BF16), ((lax.axis_size(FIRST), 2, DH), F32)],
        [VMEM] * 2,
    )(pieces, d_local)
    arrived = step(behind, ("zh", "y"), -1)
    gains = lax.all_to_all(gains, FIRST, 0, 0)
    (gains,) = call(relay_kernel, [((lax.axis_size(SECOND), 2, DH), F32)], [VMEM])(gains)
    gains = lax.all_to_all(gains, SECOND, 0, 0)
    d_k_raw, d_values, d_q_gain, d_k_gain = call(
        last_kernel,
        [((TOK * KV, DH), BF16), ((TOK * KV, DH), BF16), ((DH,), F32), ((DH,), F32)],
        [VMEM] * 5,
    )(own, arrived, k_own, k_gain, gains)
    return (d_q_raw, d_k_raw.reshape(TOK, KV, DH), d_values.reshape(TOK, KV, DH),
            d_q_gain, d_k_gain)


def solution(mesh):
    devices = np.asarray(mesh.devices).reshape(4, 8, 4, 2, 2)
    mesh = jax.sharding.Mesh(devices, ("zh", "y", "x", "zl", "c"))
    rows = ("zh", "y", "x")
    heads = ("zl", "c")
    placed = P(rows, heads, None)
    return jax.shard_map(
        per_device,
        mesh=mesh,
        in_specs=(placed,) * 5 + (P(heads, rows), P(), P(), P()),
        out_specs=(placed,) * 3 + (P(), P()),
        check_vma=False,
    )
```

```python
import jax
import jax.numpy as jnp
import numpy as np
from jax import lax
from jax.experimental import pallas as pl
from jax.experimental.pallas import tpu as pltpu
from jax.sharding import PartitionSpec as P

F32 = jnp.float32
BF16 = jnp.bfloat16
EPSILON = 1e-06
TOK = 128
HALF = 64
KV = 2
MEM = 8
DH = 128
ROWS = HALF * MEM
SLOTS = 4
SCALE = DH ** (-0.5)
LOG2E = float(np.log2(np.e))
PAYLOAD = 2 * TOK * KV
EXTRA = 16
BUILD_SIZE = 1 << 20
STATS = PAYLOAD + 8
FIRST = ("y", "c")
SECOND = ("zh", "zl")
ANY = pl.BlockSpec(memory_space=pl.ANY)
VMEM = pl.BlockSpec(memory_space=pltpu.VMEM)
SMEM = pl.BlockSpec(memory_space=pltpu.SMEM)
PARAMS = pltpu.CompilerParams(vmem_limit_bytes=12 * 1024 * 1024)


def facts(spans):
    block = (lax.axis_index("zh") * 8 + lax.axis_index("y")) * SLOTS + lax.axis_index("x")
    place = lax.axis_index("x")
    first, second = spans[2 * block], spans[2 * block + 1]
    flip = (first > second).astype(jnp.int32)
    early = jnp.minimum(first, second)
    wraps = [lax.rem(place - slot + SLOTS - 1, SLOTS) + 1 > early for slot in range(SLOTS)]
    return flip, place, wraps


def dot_nt(a, b):
    return lax.dot_general(a, b, (((1,), (1,)), ((), ())), preferred_element_type=F32)


def dot_nn(a, b):
    return lax.dot_general(a, b, (((1,), (0,)), ((), ())), preferred_element_type=F32)


def dot_tn(a, b):
    return lax.dot_general(a, b, (((0,), (0,)), ((), ())), preferred_element_type=F32)


def unit_of(floats):
    inverse = lax.rsqrt(jnp.mean(floats * floats, axis=-1, keepdims=True) + EPSILON)
    return floats * inverse, inverse


def norm_backward(unit, inverse, gain, gradient):
    scaled = gradient * gain
    projected = jnp.mean(scaled * unit, axis=-1, keepdims=True)
    return (scaled - unit * projected) * inverse


def pair(key, value, query, grad_out, lse2, delta, mask=None, keep=None):
    scores = dot_nt(key, query)
    probs = jnp.exp2(scores * (SCALE * LOG2E) - lse2)
    if mask is not None:
        probs = jnp.where(mask, probs, 0.0)
    if keep is not None:
        probs = jnp.concatenate([jnp.where(flag, probs[slot * HALF:(slot + 1) * HALF], 0.0)
                                 for slot, flag in enumerate(keep)], axis=0)
    d_probs = dot_nt(value, grad_out)
    d_scores = (probs * (d_probs - delta)).astype(BF16)
    d_value = dot_nn(probs.astype(BF16), grad_out)
    d_key = dot_nn(d_scores, query) * SCALE
    d_query = dot_tn(d_scores, key) * SCALE
    return d_query, d_key, d_value


def split(scratch, at, group):
    first = scratch[at, pl.ds(group, HALF, stride=KV), :].astype(BF16)
    second = scratch[at, pl.ds(TOK + group, HALF, stride=KV), :].astype(BF16)
    return first, second


def prep_kernel(spans, q_raw, d_out, attn_out, lse2, k_raw, values, q_gain, k_gain,
                q_norm, grads_out, d_query, d_local, keys, made, stats):
    flip, _, wrapped = facts(spans)
    flipped = flip == 1
    gain = q_gain[...].reshape(1, DH)
    ones = jnp.ones((8, DH), BF16)
    for group in range(KV):
        q_rows = q_raw[...].astype(F32)[:, group * MEM:(group + 1) * MEM, :]
        unit, _ = unit_of(q_rows.reshape(TOK * MEM, DH))
        normed = (unit * gain).astype(BF16)
        grads = d_out[...].astype(F32)[:, group * MEM:(group + 1) * MEM, :].reshape(TOK * MEM, DH)
        outs = attn_out[...].astype(F32)[:, group * MEM:(group + 1) * MEM, :].reshape(TOK * MEM, DH)
        row_delta = sum(dot_nt(ones, term.astype(BF16)) for term in three_terms(grads * outs))
        grads = grads.astype(BF16)
        for half in range(2):
            rows = slice(half * ROWS, (half + 1) * ROWS)
            q_norm[group, half] = normed[rows]
            grads_out[group, half] = grads[rows]
            stats[group, half, 0:1] = lse2[group, half]
            stats[group, half, 1:2] = row_delta[0:1, rows]

    k_unit, _ = unit_of(k_raw[...].astype(F32))
    keys[0] = (k_unit * k_gain[...].reshape(1, DH)).astype(BF16).astype(F32)
    keys[1] = values[...].astype(F32)
    key_at = lax.broadcasted_iota(jnp.int32, (HALF, ROWS), 0)
    query_at = lax.broadcasted_iota(jnp.int32, (HALF, ROWS), 1) // MEM
    mask = key_at <= query_at
    late = 1 - flip
    for group in range(KV):
        key = split(keys, 0, group)
        value = split(keys, 1, group)
        d_key = []
        d_value = []
        for half in range(2):
            dq, dk, dv = pair(key[half], value[half], q_norm[group, half], grads_out[group, half],
                              stats[group, half, 0:1], stats[group, half, 1:2], mask)
            d_query[group, half] = dq
            d_key.append(dk)
            d_value.append(dv)
        early_key = jnp.where(flipped, key[1], key[0])
        early_value = jnp.where(flipped, value[1], value[0])
        dq, dk, dv = pair(early_key, early_value, q_norm[group, late], grads_out[group, late],
                          stats[group, late, 0:1], stats[group, late, 1:2])
        d_query[group, late] += dq
        for half in range(2):
            here = flipped if half == 1 else jnp.logical_not(flipped)
            rows = pl.ds(half * TOK + group, HALF, stride=KV)
            made[0, rows, :] = d_key[half] + jnp.where(here, dk, 0.0)
            made[1, rows, :] = d_value[half] + jnp.where(here, dv, 0.0)
    for group in range(KV):
        for half in range(2):
            base = STATS + (group * 2 + half) * 8
            for part in range(4):
                lanes = slice(part * DH, (part + 1) * DH)
                d_local[base + part:base + part + 1] = stats[group, half, 0:1, lanes]
                d_local[base + 4 + part:base + 5 + part] = stats[group, half, 1:2, lanes]
    d_local[0:TOK * KV] = made[0]
    d_local[TOK * KV:PAYLOAD] = made[1]
    flags = [jnp.full((1, DH), flag, jnp.int32).astype(F32) for flag in [flip] + [w.astype(jnp.int32) for w in wrapped]]
    d_local[PAYLOAD:PAYLOAD + 8] = jnp.concatenate(
        [jnp.sum(made[0] * k_unit, axis=0, keepdims=True), gain, k_gain[...].reshape(1, DH)] + flags, axis=0)


def build_kernel(k_own, v_own, k_behind, v_behind, out, sems):
    place = lax.axis_index("x")
    for slot in range(SLOTS):
        for which, (own, behind) in enumerate(((k_own, k_behind), (v_own, v_behind))):
            target = out.at[slot, pl.ds(which * TOK * KV, TOK * KV)]

            @pl.when(slot > place)
            def _():
                pltpu.make_async_copy(own, target, sems.at[slot, which]).start()

            @pl.when(slot <= place)
            def _():
                pltpu.make_async_copy(behind, target, sems.at[slot, which]).start()

    for slot in range(SLOTS):
        for which in range(2):
            target = out.at[slot, pl.ds(which * TOK * KV, TOK * KV)]
            pltpu.make_async_copy(k_behind, target, sems.at[slot, which]).wait()


def three_terms(floats):
    high = floats.astype(BF16).astype(F32)
    rest = floats - high
    middle = rest.astype(BF16).astype(F32)
    return [high, middle, rest - middle]


def main_kernel(blocks, q_norm, grads_out, d_query0, q_raw, d_local,
                d_q_raw, pieces, d_query, units, keys, vals, grads, sums, d_q_rows, sems):
    q_gain, k_gain = d_local[PAYLOAD + 1:PAYLOAD + 2], d_local[PAYLOAD + 2:PAYLOAD + 3]
    flags = [jnp.max(d_local[PAYLOAD + at:PAYLOAD + at + 1]).astype(jnp.int32) for at in range(3, 8)]
    flip, wrapped = flags[0], [flag == 1 for flag in flags[1:]]
    flipped = flip == 1
    late = 1 - flip
    inside = [jnp.logical_not(flag) for flag in wrapped]
    some_inside = inside[0] | inside[1] | inside[2] | inside[3]
    some_wrapped = wrapped[0] | wrapped[1] | wrapped[2] | wrapped[3]
    for slot in range(SLOTS):
        unit, _ = unit_of(blocks[slot, 0:TOK * KV].astype(F32))
        units[slot] = unit
        keys[slot] = (unit * k_gain).astype(BF16).astype(F32)
        vals[slot] = blocks[slot, TOK * KV:PAYLOAD].astype(F32)

    def stats(group, half):
        rows = d_local[pl.ds(pl.multiple_of(STATS + (group * 2 + half) * 8, 8), 8), :]
        return [jnp.concatenate([rows[at + part:at + part + 1] for part in range(4)], axis=1) for at in (0, 4)]

    early_keys, early_values = [], []

    def gather(scratch, group, want_late):
        halves = [split(scratch, slot, group) for slot in range(SLOTS)]
        first = flipped if want_late else jnp.logical_not(flipped)
        return jnp.concatenate([jnp.where(first, half[0], half[1]) for half in halves], axis=0)

    def finish(half, q_sum):
        raw = q_raw[pl.ds(pl.multiple_of(half * HALF, HALF), HALF)].astype(F32)
        made = []
        for group in range(KV):
            unit, inverse = unit_of(raw[:, group * MEM:(group + 1) * MEM, :].reshape(ROWS, DH))
            gradient = d_query[group, half]
            q_sum += jnp.sum(gradient * unit, axis=0, keepdims=True)
            made.append(norm_backward(unit, inverse, q_gain, gradient).reshape(HALF, MEM, DH))
        tokens = pl.ds(pl.multiple_of(half * HALF, HALF), HALF)
        d_q_rows[tokens] = jnp.concatenate(made, axis=1).astype(BF16)
        return q_sum, tokens

    for group in range(KV):
        early_keys.append(gather(keys, group, False))
        early_values.append(gather(vals, group, False))
        d_query[group, flip] = d_query0[group, flip]
        for at in range(4):
            sums[group, at] = jnp.zeros((SLOTS * HALF, DH), F32)

        @pl.when(some_inside)
        def _():
            dq, dk, dv = pair(early_keys[group], early_values[group], q_norm[group, flip], grads_out[group, flip],
                              *stats(group, flip), keep=inside)
            d_query[group, flip] += dq
            sums[group, 0] = dk
            sums[group, 1] = dv

    q_sum, tokens = finish(flip, jnp.zeros((1, DH), F32))
    early_copy = pltpu.make_async_copy(d_q_rows.at[tokens], d_q_raw.at[tokens], sems.at[0])
    early_copy.start()
    for group in range(KV):
        dq, dk, dv = pair(early_keys[group], early_values[group], q_norm[group, late], grads_out[group, late],
                          *stats(group, late))
        d_query[group, late] = d_query0[group, late] + dq
        sums[group, 0] += dk
        sums[group, 1] += dv

        @pl.when(some_wrapped)
        def _():
            dq, dk, dv = pair(gather(keys, group, True), gather(vals, group, True), q_norm[group, late],
                              grads_out[group, late], *stats(group, late), keep=wrapped)
            d_query[group, late] += dq
            sums[group, 2] = dk
            sums[group, 3] = dv

    q_sum, tokens = finish(late, q_sum)
    late_copy = pltpu.make_async_copy(d_q_rows.at[tokens], d_q_raw.at[tokens], sems.at[1])
    late_copy.start()
    for group in range(KV):
        for slot in range(SLOTS):
            span = slice(slot * HALF, (slot + 1) * HALF)
            for which in range(2):
                of_early, of_late = sums[group, which, span], sums[group, 2 + which, span]
                at = slot * 2 + which
                grads[at, pl.ds(group, HALF, stride=KV), :] = jnp.where(flipped, of_late, of_early)
                grads[at, pl.ds(TOK + group, HALF, stride=KV), :] = jnp.where(flipped, of_early, of_late)

    k_sum = d_local[PAYLOAD:PAYLOAD + 1]
    for slot in range(SLOTS):
        k_sum += jnp.sum(grads[2 * slot] * units[slot], axis=0, keepdims=True)
        pieces[slot, 0:TOK * KV] = grads[2 * slot].astype(BF16)
        pieces[slot, TOK * KV:PAYLOAD] = grads[2 * slot + 1].astype(BF16)

    terms = three_terms(q_sum) + three_terms(k_sum) + [jnp.zeros((EXTRA - 6, DH), F32)]
    extra = jnp.concatenate(terms, axis=0).astype(BF16)
    for slot in range(SLOTS):
        pieces[slot, PAYLOAD:PAYLOAD + EXTRA] = extra
    early_copy.wait()
    late_copy.wait()


def sum_kernel(pieces, d_local, own, behind, gains):
    place = lax.axis_index("x")
    total = d_local[0:PAYLOAD]
    others = jnp.zeros((PAYLOAD, DH), F32)
    extra = jnp.zeros((EXTRA, DH), F32)
    for slot in range(SLOTS):
        piece = pieces[slot, 0:PAYLOAD].astype(F32)
        ahead = slot > place
        total += jnp.where(ahead, piece, 0.0)
        others += jnp.where(ahead, 0.0, piece)
        extra += pieces[slot, PAYLOAD:PAYLOAD + EXTRA].astype(F32)
    own[...] = total
    behind[...] = others.astype(BF16)
    both = jnp.concatenate([jnp.sum(extra[0:3], axis=0, keepdims=True), jnp.sum(extra[3:6], axis=0, keepdims=True)], axis=0)
    for peer in range(gains.shape[0]):
        gains[peer] = both


def relay_kernel(gathered, spread):
    both = jnp.sum(gathered[...], axis=0)
    for peer in range(spread.shape[0]):
        spread[peer] = both


def last_kernel(own, arrived, k_raw, k_gain, gathered, d_k_raw, d_values, q_sum, k_sum):
    total = own[...] + arrived[...].astype(F32)
    unit, inverse = unit_of(k_raw[...].astype(F32))
    d_k_raw[...] = norm_backward(unit, inverse, k_gain[...].reshape(1, DH), total[0:TOK * KV]).astype(BF16)
    d_values[...] = total[TOK * KV:PAYLOAD].astype(BF16)
    both = jnp.sum(gathered[...], axis=0)
    q_sum[...] = both[0]
    k_sum[...] = both[1]


def call(kernel, outs, specs, scratch=(), flops=0, size=0, out_specs=None):
    return pl.pallas_call(
        kernel,
        out_shape=[jax.ShapeDtypeStruct(*o) for o in outs],
        in_specs=specs,
        out_specs=out_specs or [VMEM] * len(outs),
        scratch_shapes=list(scratch),
        compiler_params=PARAMS,
        cost_estimate=pl.CostEstimate(flops=flops, bytes_accessed=size, transcendentals=0),
    )


def step(block, axes, distance):
    size = lax.axis_size(axes)
    return lax.ppermute(block, axes, [((i - distance) % size, i) for i in range(size)])


def per_device(q_raw, k_raw, values, attn_out, d_out, lse, q_gain, k_gain, span_order):
    k_own = k_raw.reshape(TOK * KV, DH)
    v_own = values.reshape(TOK * KV, DH)
    k_behind = step(k_own, ("zh", "y"), 1)
    v_behind = step(v_own, ("zh", "y"), 1)

    lse2 = (lse * LOG2E).reshape(KV, MEM, TOK).transpose(0, 2, 1).reshape(KV, 2, 1, ROWS)

    q_norm, grads_out, d_query0, d_local = call(
        prep_kernel,
        [((KV, 2, ROWS, DH), BF16), ((KV, 2, ROWS, DH), BF16),
         ((KV, 2, ROWS, DH), F32), ((STATS + KV * 2 * 8, DH), F32)],
        [SMEM] + [VMEM] * 8,
        [pltpu.VMEM((2, TOK * KV, DH), F32)] * 2 + [pltpu.VMEM((KV, 2, 8, ROWS), F32)],
        flops=int(6e9), size=1 << 22,
    )(span_order, q_raw, d_out, attn_out, lse2, k_own, v_own, q_gain, k_gain)

    (blocks,) = call(build_kernel, [((SLOTS, PAYLOAD, DH), BF16)], [VMEM] * 4, [pltpu.SemaphoreType.DMA((SLOTS, 2))],
                     size=BUILD_SIZE, out_specs=[ANY])(k_own, v_own, k_behind, v_behind)
    blocks = lax.all_to_all(blocks, "x", 0, 0)
    d_q_raw, pieces = call(
        main_kernel,
        [((TOK, KV * MEM, DH), BF16), ((SLOTS, PAYLOAD + EXTRA, DH), BF16)],
        [VMEM] * 6,
        [pltpu.VMEM((KV, 2, ROWS, DH), F32)] + [pltpu.VMEM((SLOTS, TOK * KV, DH), F32)] * 3
        + [pltpu.VMEM((2 * SLOTS, TOK * KV, DH), F32), pltpu.VMEM((KV, 4, SLOTS * HALF, DH), F32),
           pltpu.VMEM((TOK, KV * MEM, DH), BF16), pltpu.SemaphoreType.DMA((2,))],
        out_specs=[ANY, VMEM],
    )(blocks, q_norm, grads_out, d_query0, q_raw, d_local)
    pieces = lax.all_to_all(pieces, "x", 0, 0)
    own, behind, gains = call(
        sum_kernel,
        [((PAYLOAD, DH), F32), ((PAYLOAD, DH), BF16), ((lax.axis_size(FIRST), 2, DH), F32)],
        [VMEM] * 2,
    )(pieces, d_local)
    arrived = step(behind, ("zh", "y"), -1)
    gains = lax.all_to_all(gains, FIRST, 0, 0)
    (gains,) = call(relay_kernel, [((lax.axis_size(SECOND), 2, DH), F32)], [VMEM])(gains)
    gains = lax.all_to_all(gains, SECOND, 0, 0)
    d_k_raw, d_values, d_q_gain, d_k_gain = call(
        last_kernel,
        [((TOK * KV, DH), BF16), ((TOK * KV, DH), BF16), ((DH,), F32), ((DH,), F32)],
        [VMEM] * 5,
    )(own, arrived, k_own, k_gain, gains)
    return (d_q_raw, d_k_raw.reshape(TOK, KV, DH), d_values.reshape(TOK, KV, DH),
            d_q_gain, d_k_gain)


def solution(mesh):
    devices = np.asarray(mesh.devices).reshape(4, 8, 4, 2, 2)
    mesh = jax.sharding.Mesh(devices, ("zh", "y", "x", "zl", "c"))
    rows = ("zh", "y", "x")
    heads = ("zl", "c")
    placed = P(rows, heads, None)
    return jax.shard_map(
        per_device,
        mesh=mesh,
        in_specs=(placed,) * 5 + (P(heads, rows), P(), P(), P()),
        out_specs=(placed,) * 3 + (P(), P()),
        check_vma=False,
    )
```
